512 devices in a mesh: section: 16 (over y, z_hi), dp: 16 (over z_lo, x), cores: 2 (over core).
Axes of the slice: x: 4, y: 8, z: 8 (z_hi: 2, z_lo: 4; z = z_hi * 4 + z_lo), core: 2. Of those that a mesh axis runs over, the one named last changes fastest.
Arguments:
- arrivals: bfloat16 [2, 1536, 2048], P(None, 'dp'), may hold values from -6 to 6
- in_flight: bfloat16 [16, 1536, 2048], P('section', 'dp'), may hold values from -6 to 6
- cotangent: bfloat16 [2, 1536, 2048], P(None, 'dp'), may hold values from -6 to 6
- grad_flight: bfloat16 [16, 1536, 2048], P('section', 'dp'), may hold values from -6 to 6
- stashed: bfloat16 [16, 2, 1536, 2048], P('section', None, 'dp'), may hold values from -6 to 6
- in_weight: bfloat16 [16, 2048, 4096], P('section', 'dp', 'cores'), may hold values from -0.125 to 0.125
- out_weight: bfloat16 [16, 1024, 2048], P('section', 'cores', 'dp'), may hold values from -0.1875 to 0.1875
- forward_blocks: int32 [16, 17], P('dp'), may hold values from 1 to 4, 42 in all within a row
- backward_blocks: int32 [16, 17], P('dp'), may hold values from 1 to 4, 42 in all within a row
- forward_marks: int32 [16, 17, 4, 4], P('dp'), may hold values 0 or 1
- backward_marks: int32 [16, 17, 4, 4], P('dp'), may hold values 0 or 1
Outputs:
- activations: bfloat16 [16, 2, 1536, 2048], P('section', None, ('dp', 'cores'))
- input_grads: bfloat16 [16, 2, 1536, 2048], P('section', None, ('dp', 'cores'))
- weight_grads: float32 [16, 1024, 2048], P('section', 'cores', 'dp')
The draws below stay inside these ranges and needn't reach their ends.
Inputs may be any that keep to these rules, and one draw needn't show every extreme that they name: `forward_blocks`: in each replica's row the 17 lengths add up to 42 blocks and the longest is 4. `backward_blocks`: in each replica's row the 17 lengths add up to 42 blocks and the longest is 4.
All inputs are finite; a program needn't handle non-finite values. No bound on the sum of `forward_marks` or of `backward_marks` on one device may be relied on, other than what follows from the above.
Results may differ from the reference program's by a relative error of at most 0.03.
Values may be sent and summed in bfloat16 or wider, within the bound.
A program may use at most 64 MiB of HBM per device.

```python
import math
import jax
import jax.numpy as jnp
import numpy as np
from jax import lax

D = 2048
HEAD_DIM = 128
BLOCK = 24
BLOCKS = 4
TICKS = 2
LAYERS = 16
ROWS = 1536
PROJ_WIDTH = 4096
ATTN_WIDTH = 1024
BATCHES = 17
TOTAL_BLOCKS = 42
N_DP = 16
N_CORES = 2


def with_ends(result, own_key, low, largest):
    extent = result.shape
    index_at = [jax.random.randint(jax.random.fold_in(own_key, axis), (), 0, extent[axis]) for axis in range(len(extent))]
    result = result.at[tuple(index_at)].set(low)
    longest = extent.index(max(extent))
    index_at[longest] = (index_at[longest] + 1) % extent[longest]
    return result.at[tuple(index_at)].set(largest)


def spiked(drawn, rng, source, target, blocks, factor):
    def block_of(dim):
        return (jnp.arange(drawn.shape[dim]) // (drawn.shape[dim] // blocks)).reshape((-1,) + (1,) * (drawn.ndim - 1 - dim))

    one_side = jax.random.permutation(rng, blocks)[block_of(target)]
    far = (block_of(target) + blocks // 2) % blocks
    return jnp.where((block_of(source) == one_side) | (block_of(source) == far), factor * drawn, drawn)


def steps_of(stream_key, shape, cuts, low, largest):
    def one(dim, blocks):
        heights = jax.random.uniform(jax.random.fold_in(jax.random.fold_in(stream_key, 6), dim), (blocks,), jnp.float32, low / len(cuts), largest / len(cuts))
        return jnp.repeat(jnp.exp(heights), shape[dim] // blocks).reshape((-1,) + (1,) * (len(shape) - dim - 1))

    factor_of = one(*cuts[0])
    for cut in cuts[1:]:
        factor_of = factor_of * one(*cut)
    return factor_of


def split_up(number_of, total, most, lean):
    portions = [(1 << 20) // math.isqrt(standing ** lean) + 1 for standing in range(2, number_of + 1)]
    spare, holding = total - most - (number_of - 1), [1] * (number_of - 1)
    while spare > 0:
        free = [i for i in range(number_of - 1) if holding[i] < most]
        pool, budget = sum([portions[i] for i in free]), spare
        for i in free:
            extra = min(most - holding[i], max(1, budget * portions[i] // pool), spare)
            holding[i] = holding[i] + extra
            spare = spare - extra
    return np.array([most] + holding)


def uneven_parts(stream_key, count, total, bound, lean):
    if count == 2:
        one = jax.random.randint(stream_key, (), max(1, total - bound), min(bound, total - 1) + 1)
        return jnp.stack([one, total - one])
    tallies = jnp.asarray(split_up(count, total, bound, lean), jnp.int32)
    couples = (count - 1) // 2
    giver, sink = tallies[1:1 + 2 * couples:2], tallies[2:2 + 2 * couples:2]
    margin = jnp.minimum(giver - 1, bound - sink)
    passed = jax.random.randint(jax.random.fold_in(stream_key, 1), (couples,), 0, 1 << 20) % (margin + 1)
    tallies = tallies.at[1:1 + 2 * couples:2].set(giver - passed).at[2:2 + 2 * couples:2].set(sink + passed)
    return tallies[jax.random.permutation(jax.random.fold_in(stream_key, 2), count)]


def scatter_about(own_key, extent, deviation, most, cuts=(), kind=jnp.bfloat16):
    level = steps_of(own_key, extent, cuts, -0.22, 0.18) if cuts else 1.0
    entries = jax.random.normal(own_key, extent, jnp.float32) * deviation * level
    return jnp.minimum(jnp.maximum(entries, -most), most).astype(kind)


def noise_with(own_key, shape, scale, limit, shards, heavy, kind=jnp.bfloat16):
    values = scale * jax.random.normal(own_key, shape, jnp.float32)
    if shards:
        values = values * steps_of(own_key, shape, shards, -0.22, 0.18)
    return jnp.clip(spiked(values, jax.random.fold_in(own_key, 3), *heavy), -limit, limit).astype(kind)


def setup_inputs(seed: int = 0) -> dict:
    splits = jax.random.split(jax.random.key(seed), 12)
    arrivals = scatter_about(splits[0], (TICKS, ROWS, D), 1.0, 6.0, ((1, 16),))
    in_flight = scatter_about(splits[1], (LAYERS, ROWS, D), 1.0, 6.0, ((0, 16), (1, 16)))
    cotangent = noise_with(splits[2], (TICKS, ROWS, D), 1.0, 6.0, ((1, 16),), (1, 2, 16, 2.0))
    grad_flight = noise_with(splits[3], (LAYERS, ROWS, D), 1.0, 6.0, ((0, 16), (1, 16)), (1, 2, 16, 2.0))
    stashed = scatter_about(splits[4], (LAYERS, TICKS, ROWS, D), 1.0, 6.0, ((0, 16), (2, 16)))
    in_weight = scatter_about(splits[5], (LAYERS, D, PROJ_WIDTH), D ** -0.5, 0.125, ((0, 16), (1, 16), (2, 2)))
    out_weight = scatter_about(splits[6], (LAYERS, ATTN_WIDTH, D), ATTN_WIDTH ** -0.5, 0.1875, ((0, 16), (1, 2), (2, 16)))
    forward_blocks = jax.vmap(lambda own: uneven_parts(own, BATCHES, TOTAL_BLOCKS, BLOCKS, 2))(jax.random.split(splits[7], N_DP)).reshape((N_DP, BATCHES)).astype(jnp.int32)
    backward_blocks = jax.vmap(lambda own: uneven_parts(own, BATCHES, TOTAL_BLOCKS, BLOCKS, 2))(jax.random.split(splits[8], N_DP)).reshape((N_DP, BATCHES)).astype(jnp.int32)
    forward_marks = with_ends((jax.random.randint(splits[9], (N_DP, BATCHES, BLOCKS, BLOCKS), 0, 2) < 1).astype(jnp.int32), jax.random.fold_in(splits[9], 1), 0, 1)
    backward_marks = with_ends((jax.random.randint(splits[10], (N_DP, BATCHES, BLOCKS, BLOCKS), 0, 2) < 1).astype(jnp.int32), jax.random.fold_in(splits[10], 1), 0, 1)
    return dict(arrivals=arrivals, in_flight=in_flight, cotangent=cotangent, grad_flight=grad_flight, stashed=stashed, in_weight=in_weight, out_weight=out_weight, forward_blocks=forward_blocks, backward_blocks=backward_blocks, forward_marks=forward_marks, backward_marks=backward_marks)


EPSILON = 1e-06

def block_keep(live_blocks, block_marks):
    length = BLOCKS * BLOCK
    places = jnp.arange(length, dtype=jnp.int32)
    owners = places // BLOCK
    onehot = (owners[:, None] == jnp.arange(BLOCKS, dtype=jnp.int32)[None, :]).astype(jnp.float32)
    spread = jnp.einsum('ia,rab,jb->rij', onehot, block_marks.astype(jnp.float32), onehot)
    allowed = (owners[:, None] == owners[None, :])[None] | (spread > 0.5)
    causal = (places[:, None] >= places[None, :])[None]
    tokens_live = live_blocks * BLOCK
    living = places[None, :] < tokens_live[:, None]
    keeping = causal & allowed & living[:, :, None] & living[:, None, :]
    return (keeping.astype(jnp.float32), 1.0 / tokens_live.astype(jnp.float32))

def norm_rows(values_f):
    return lax.rsqrt(lax.optimization_barrier(jnp.mean(values_f * values_f, axis=-1, keepdims=True)) + EPSILON)

def heads_forward(pre_act, keeping, inverse_count):
    scaling = HEAD_DIM ** (-0.5)
    active = jax.nn.silu(pre_act)
    gate_rows = active[:, :, :, 0]
    value_rows = active[:, :, :, 1].astype(jnp.bfloat16)
    query_rows = active[:, :, :, 2].astype(jnp.bfloat16)
    key_rows = active[:, :, :, 3].astype(jnp.bfloat16)
    scores = jnp.einsum('rigd,rjgd->rgij', query_rows.astype(jnp.float32), key_rows.astype(jnp.float32)) * scaling
    weights = keeping[:, None] * inverse_count[:, None, None, None]
    attention = (jax.nn.silu(scores) * weights).astype(jnp.bfloat16)
    mixed = jnp.einsum('rgij,rjgd->rigd', attention.astype(jnp.float32), value_rows.astype(jnp.float32))
    root_scale = lax.rsqrt(lax.optimization_barrier(jnp.mean(mixed * mixed, axis=-1, keepdims=True)) + EPSILON)
    normed = mixed * root_scale
    gated = (normed * gate_rows).astype(jnp.bfloat16)
    return (gated, (gate_rows, value_rows, query_rows, key_rows, scores, weights, attention, root_scale, normed))

def heads_backward(pre_act, saved, upstream):
    gate_rows, value_rows, query_rows, key_rows, scores, weights, attention, root_scale, normed = saved
    scaling = HEAD_DIM ** (-0.5)
    grad_gated = upstream.astype(jnp.float32)
    grad_normed = grad_gated * gate_rows
    grad_gate = grad_gated * normed
    grad_mixed = root_scale * (grad_normed - normed * lax.optimization_barrier(jnp.mean(grad_normed * normed, axis=-1, keepdims=True)))
    mixed_low = grad_mixed.astype(jnp.bfloat16)
    grad_attention = jnp.einsum('rigd,rjgd->rgij', mixed_low.astype(jnp.float32), value_rows.astype(jnp.float32))
    grad_value = jnp.einsum('rgij,rigd->rjgd', attention.astype(jnp.float32), mixed_low.astype(jnp.float32))
    sigmoid_s = jax.nn.sigmoid(scores)
    grad_scores = (grad_attention * weights * sigmoid_s * (1.0 + scores * (1.0 - sigmoid_s)) * scaling).astype(jnp.bfloat16)
    grad_query = jnp.einsum('rgij,rjgd->rigd', grad_scores.astype(jnp.float32), key_rows.astype(jnp.float32))
    grad_key = jnp.einsum('rgij,rigd->rjgd', grad_scores.astype(jnp.float32), query_rows.astype(jnp.float32))
    grad_active = jnp.stack([grad_gate, grad_value, grad_query, grad_key], axis=3)
    sigmoid_u = jax.nn.sigmoid(pre_act)
    return (grad_active * sigmoid_u * (1.0 + pre_act * (1.0 - sigmoid_u))).astype(jnp.bfloat16)

def section_forward(inputs, in_matrix, out_matrix, keeping, inverse_count):
    replicas, length, width = inputs.shape
    floats = inputs.astype(jnp.float32)
    normed_low = (floats * norm_rows(floats)).astype(jnp.bfloat16).reshape(replicas * length, width)
    columns = in_matrix.shape[1] // N_CORES
    slab_rows = out_matrix.shape[0] // N_CORES
    groups = slab_rows // HEAD_DIM
    summed = floats
    for core_no in range(N_CORES):
        pre_act = jnp.dot(normed_low, in_matrix[:, core_no * columns:(core_no + 1) * columns], preferred_element_type=jnp.float32)
        gated, unused = heads_forward(pre_act.reshape(replicas, length, groups, 4, HEAD_DIM), keeping, inverse_count)
        partial_sum = jnp.dot(gated.reshape(replicas * length, slab_rows), out_matrix[core_no * slab_rows:(core_no + 1) * slab_rows], preferred_element_type=jnp.float32)
        summed = summed + lax.optimization_barrier(partial_sum.astype(jnp.bfloat16)).astype(jnp.float32).reshape(replicas, length, width)
    return summed.astype(jnp.bfloat16)

def section_backward(inputs, upstream, in_matrix, out_matrix, keeping, inverse_count):
    replicas, length, width = inputs.shape
    floats = inputs.astype(jnp.float32)
    root_inputs = norm_rows(floats)
    scaled = floats * root_inputs
    normed_low = scaled.astype(jnp.bfloat16).reshape(replicas * length, width)
    flat_up = upstream.reshape(replicas * length, width)
    columns = in_matrix.shape[1] // N_CORES
    slab_rows = out_matrix.shape[0] // N_CORES
    groups = slab_rows // HEAD_DIM
    summed = upstream.astype(jnp.float32)
    products = []
    for core_no in range(N_CORES):
        in_slab = in_matrix[:, core_no * columns:(core_no + 1) * columns]
        out_slab = out_matrix[core_no * slab_rows:(core_no + 1) * slab_rows]
        pre_act = jnp.dot(normed_low, in_slab, preferred_element_type=jnp.float32).reshape(replicas, length, groups, 4, HEAD_DIM)
        gated, saved = heads_forward(pre_act, keeping, inverse_count)
        grad_gated = jnp.dot(flat_up, out_slab.T, preferred_element_type=jnp.float32).astype(jnp.bfloat16).reshape(replicas, length, groups, HEAD_DIM)
        grad_pre = heads_backward(pre_act, saved, grad_gated).reshape(replicas * length, columns)
        grad_normed = jnp.dot(grad_pre, in_slab.T, preferred_element_type=jnp.float32).reshape(replicas, length, width)
        back_part = root_inputs * (grad_normed - scaled * lax.optimization_barrier(jnp.mean(grad_normed * scaled, axis=-1, keepdims=True)))
        summed = summed + lax.optimization_barrier(back_part.astype(jnp.bfloat16)).astype(jnp.float32)
        products.append(jnp.einsum('rsf,rsd->rfd', gated.reshape(replicas, length, slab_rows).astype(jnp.float32), upstream.astype(jnp.float32)))
    return (summed.astype(jnp.bfloat16), jnp.concatenate(products, axis=1))

def reference(arrivals, in_flight, cotangent, grad_flight, stashed, in_weight, out_weight, forward_blocks, backward_blocks, forward_marks, backward_marks):
    ticks = arrivals.shape[0]
    rows = arrivals.shape[1]
    width = arrivals.shape[2]
    sections = in_flight.shape[0]
    length = BLOCKS * BLOCK
    replicas = rows // length

    def split(values):
        return values.reshape(replicas, length, width)
    outputs = [[None] * ticks for index in range(sections)]
    for section_no in range(sections):
        for tick_no in range(ticks):
            if section_no == 0:
                inputs = arrivals[tick_no]
            elif tick_no == 0:
                inputs = in_flight[section_no]
            else:
                inputs = outputs[section_no - 1][tick_no - 1]
            history = tick_no - section_no + sections - 1
            keeping, inverse_count = block_keep(forward_blocks[:, history], forward_marks[:, history])
            outputs[section_no][tick_no] = section_forward(split(inputs), in_weight[section_no], out_weight[section_no], keeping, inverse_count).reshape(rows, width)
    backs = [[None] * ticks for index in range(sections)]
    grads_list = [None] * sections
    scaling = (ticks * rows) ** (-0.5)
    for section_no in reversed(range(sections)):
        running = jnp.zeros((replicas, out_weight.shape[1], width), jnp.float32)
        for tick_no in range(ticks):
            if section_no == sections - 1:
                upstream = cotangent[tick_no]
            elif tick_no == 0:
                upstream = grad_flight[section_no]
            else:
                upstream = backs[section_no + 1][tick_no - 1]
            history = tick_no + section_no
            keeping, inverse_count = block_keep(backward_blocks[:, history], backward_marks[:, history])
            grad_in, product = section_backward(split(stashed[section_no, tick_no]), split(upstream), in_weight[section_no], out_weight[section_no], keeping, inverse_count)
            backs[section_no][tick_no] = grad_in.reshape(rows, width)
            running = running + product
        rounded = lax.optimization_barrier(running.astype(jnp.bfloat16)).astype(jnp.float32)
        grads_list[section_no] = lax.optimization_barrier(jnp.sum(rounded, axis=0)) * scaling
    activations = jnp.stack([jnp.stack(outputs[index]) for index in range(sections)])
    input_grads = jnp.stack([jnp.stack(backs[index]) for index in range(sections)])
    return (activations, input_grads, jnp.stack(grads_list))
```

```python
import jax
import jax.numpy as jnp
from jax import lax
from jax.experimental import pallas as pl
from jax.experimental.pallas import tpu as pltpu
from jax.sharding import PartitionSpec as P

HEAD = 128
HEADS = 4
WIDE = 4 * HEAD
BLOCK = 24
BLOCKS = 4
ROWS = BLOCK * BLOCKS
HALF = ROWS // 2
D = 2048
TICKS = 2
NZ, NX = 4, 4
NDP = NZ * NX
SHARD = D // NDP
EPSILON = 1e-06
SCALE = HEAD**-0.5
MESH = pl.DeviceIdType.MESH
F32, BF16 = jnp.float32, jnp.bfloat16

NT = (((1,), (1,)), ((), ()))
TN = (((0,), (0,)), ((), ()))


def sigmoid(v):
    return 1.0 / (1.0 + jnp.exp(-v))


def dot(a, b, dims=(((1,), (0,)), ((), ()))):
    return lax.dot_general(a, b, dims, preferred_element_type=F32)


def inverse_rms(v):
    return lax.rsqrt(jnp.mean(v * v, axis=-1, keepdims=True) + EPSILON)


def keep_count(blocks, marks, history):
    i = lax.broadcasted_iota(jnp.int32, (ROWS, ROWS), 0)
    j = lax.broadcasted_iota(jnp.int32, (ROWS, ROWS), 1)

    def owner(p):
        return sum((p >= BLOCK * b).astype(jnp.int32) for b in range(1, BLOCKS))

    bi, bj = owner(i), owner(j)
    spread = (bi == bj).astype(jnp.int32)
    for a in range(1, BLOCKS):
        for b in range(a):
            here = ((bi == a) & (bj == b)).astype(jnp.int32)
            spread = spread + here * marks[0, history, a, b]
    live = jnp.full((ROWS, ROWS), blocks[0, history] * BLOCK, jnp.int32)
    keep = (spread > 0) & (j <= i) & (i < live) & (j < live)
    return jnp.where(keep, 1.0 / live.astype(F32), 0.0)


def kernel(
    sections,
    arrivals,
    in_flight,
    cotangent,
    grad_flight,
    stashed,
    in_weight,
    out_weight,
    f_blocks,
    b_blocks,
    f_marks,
    b_marks,
    acts_out,
    grads_out,
    wgrad_out,
    win,
    wout,
    gat,
    gcol,
    xin,
    gin,
    xsrc,
    gsrc,
    stash,
    xn,
    u_s,
    part,
    dxn,
    dgat,
    dsil_s,
    gate_s,
    norm_s,
    rs_s,
    v_s,
    q_s,
    k_s,
    p_s,
    dsc_s,
    keep_s,
    esend,
    erecv,
    outs,
    wg_s,
    load_sem,
    ag_recv,
    ag_send,
    ex_send,
    ex_recv,
    sec_send,
    sec_recv,
    fw_send,
    fw_recv,
    a2a_send,
    a2a_recv,
    st_sem,
):
    s = lax.axis_index("section")
    me = lax.axis_index("dp")
    c = lax.axis_index("cores")
    z, x = me // NX, me % NX
    right, left, across = (x + 1) % NX, (x + NX - 1) % NX, (x + 2) % NX
    peer_z = (z + 1 - 2 * (z % 2), (z + 2) % NZ, NZ - 1 - z)
    zs = (z,) + peer_z
    ahead, behind = (s + 1) % sections, (s + sections - 1) % sections
    mine, other = pl.multiple_of(c * HALF, 16), pl.multiple_of((1 - c) * HALF, 16)

    barrier = pltpu.get_barrier_semaphore()
    for k in range(1, NDP):
        pl.semaphore_signal(barrier, inc=1, device_id=(s, (me + k) % NDP, c), device_id_type=MESH)
    pl.semaphore_signal(barrier, inc=1, device_id=(s, me, 1 - c), device_id_type=MESH)
    pl.semaphore_signal(barrier, inc=1, device_id=(ahead, me, c), device_id_type=MESH)
    pl.semaphore_signal(barrier, inc=1, device_id=(behind, me, c), device_id_type=MESH)

    def chunk(n, owner):
        if n == 2:
            return wout.at[:, pl.ds(pl.multiple_of(owner * SHARD, SHARD), SHARD)]
        if n == 5:
            return gat.at[:, owner]
        h = n if n < 2 else n - 1
        return win.at[h, pl.ds(pl.multiple_of(owner * SHARD, SHARD), SHARD), :]

    loads = []
    for h in range(HEADS):
        n = h if h < 2 else h + 1
        loads.append((in_weight.at[0, :, pl.ds(h * WIDE, WIDE)], chunk(n, me)))
    loads.append((out_weight.at[0], chunk(2, me)))
    loads += [
        (stashed.at[0], stash),
        (arrivals, xsrc),
        (in_flight.at[0], xin.at[0]),
        (cotangent, gsrc),
        (grad_flight.at[0], gin.at[0]),
    ]
    loads = [pltpu.make_async_copy(a, b, load_sem.at[i]) for i, (a, b) in enumerate(loads)]
    for copy in loads:
        copy.start()

    def remote(src, dst, send, recv, to):
        return pltpu.make_async_remote_copy(
            src_ref=src, dst_ref=dst, send_sem=send, recv_sem=recv, device_id=to, device_id_type=MESH
        )

    sent = []

    def ag(n, owner, slot, to_z, to_x):
        part_ref = chunk(n, owner)
        return remote(
            part_ref, part_ref, ag_send.at[n, slot], ag_recv.at[n, owner], (s, to_z * NX + to_x, c)
        )

    def push(n, owner, slot, to_z, to_x):
        copy = ag(n, owner, slot, to_z, to_x)
        copy.start()
        sent.append(copy)

    def arrive(n, owner):
        ag(n, owner, 0, z, right).wait_recv()

    def begin(n):
        push(n, me, 0, z, right)
        push(n, me, 1, z, left)
        for i in range(3):
            push(n, me, 2 + i, peer_z[i], x)

    def spread(n):
        for i in range(3):
            owner = peer_z[i] * NX + x
            arrive(n, owner)
            push(n, owner, 5 + 2 * i, z, right)
            push(n, owner, 6 + 2 * i, z, left)

    def forward(n):
        for i in range(4):
            from_left, from_right = zs[i] * NX + left, zs[i] * NX + right
            if i in (0, 3):
                arrive(n, from_left)
                push(n, from_left, 11 + i, z, right)
                arrive(n, from_right)
            else:
                arrive(n, from_right)
                push(n, from_right, 11 + i, z, left)
                arrive(n, from_left)

    def finish(n):
        for i in range(4):
            arrive(n, zs[i] * NX + across)

    loads[0].wait()
    pl.semaphore_wait(barrier, NDP - 1 + 3)
    begin(0)
    loads[1].wait()
    begin(1)

    for t in range(TICKS):
        keep_s[t] = keep_count(f_blocks, f_marks, t - s + sections - 1)
        keep_s[2 + t] = keep_count(b_blocks, b_marks, t + s)

    def normed(v):
        v = v.astype(F32)
        return (v * inverse_rms(v)).astype(BF16)

    spread(0)
    for copy in loads[2:]:
        copy.wait()
    begin(2)

    xsrc[0] = jnp.where(s == 0, xsrc[0], xin[0])
    gsrc[0] = jnp.where(s == sections - 1, gsrc[0], gin[0])
    xn[0:ROWS] = normed(xsrc[0])
    for t in range(TICKS):
        xn[ROWS * (t + 1) : ROWS * (t + 2)] = normed(stash[t])

    a2a_sent = []

    def a2a(t, k):
        to = (me + k) % NDP
        return remote(
            gsrc.at[t, :, pl.ds(pl.multiple_of(to * SHARD, SHARD), SHARD)],
            gcol.at[t, me],
            a2a_send.at[t, k],
            a2a_recv.at[t, me],
            (s, to, c),
        )

    def a2a_start(t):
        for k in range(1, NDP):
            copy = a2a(t, k)
            copy.start()
            a2a_sent.append(copy)
        gcol[t, me] = gsrc[t, :, pl.ds(pl.multiple_of(me * SHARD, SHARD), SHARD)]

    def a2a_wait(t):
        for k in range(1, NDP):
            sender = (me + k) % NDP
            remote(
                gsrc.at[t, :, pl.ds(0, SHARD)],
                gcol.at[t, sender],
                a2a_send.at[t, k],
                a2a_recv.at[t, sender],
                (s, sender, c),
            ).wait_recv()

    def heads_forward(u, keep):
        sg = sigmoid(u)
        act = u * sg
        gate = act[:, :HEAD]
        v = act[:, HEAD : 2 * HEAD].astype(BF16)
        q = act[:, 2 * HEAD : 3 * HEAD].astype(BF16)
        k = act[:, 3 * HEAD :].astype(BF16)
        scores = dot(q, k, NT) * SCALE
        ss = sigmoid(scores)
        probs = (scores * ss * keep).astype(BF16)
        mixed = dot(probs, v)
        rs = inverse_rms(mixed)
        norm = mixed * rs
        return (norm * gate).astype(BF16), (sg, gate, v, q, k, scores, ss, probs, rs, norm)

    def ahead_part(t, h, u):
        gated, _ = heads_forward(u, keep_s[t])
        more = dot(gated, wout[h * HEAD : (h + 1) * HEAD, :])
        if h == 0:
            part[...] = more
        else:
            part[...] += more

    def back_first(t, h, u):
        keep = keep_s[2 + t]
        gated, (sg, gate, v, q, k, scores, ss, probs, rs, norm) = heads_forward(u, keep)
        gat[t, me, :, h * HEAD : (h + 1) * HEAD] = gated
        dsil_s[t, h] = sg * (1.0 + u * (1.0 - sg))
        gate_s[t, h] = gate
        norm_s[t, h] = norm
        rs_s[t, h] = jnp.broadcast_to(rs, (ROWS, HEAD))
        v_s[t, h] = v
        q_s[t, h] = q
        k_s[t, h] = k
        p_s[t, h] = probs
        dsc_s[t, h] = keep * ss * (1.0 + scores * (1.0 - ss)) * SCALE

    def back_second(t, h):
        dg = dgat[:, h * HEAD : (h + 1) * HEAD].astype(F32)
        norm = norm_s[t, h]
        dn = dg * gate_s[t, h]
        dgate = dg * norm
        dm = (rs_s[t, h] * (dn - norm * jnp.mean(dn * norm, axis=-1, keepdims=True))).astype(BF16)
        dp = dot(dm, v_s[t, h], NT)
        dv = dot(p_s[t, h], dm, TN)
        ds = (dp * dsc_s[t, h]).astype(BF16)
        dq = dot(ds, k_s[t, h])
        dk = dot(ds, q_s[t, h], TN)
        du = (jnp.concatenate([dgate, dv, dq, dk], axis=1) * dsil_s[t, h]).astype(BF16)
        more = dot(du, win[h], NT)
        if h == 0:
            dxn[...] = more
        else:
            dxn[...] += more

    def gated_grad(t):
        dgat[...] = dot(gsrc[t], wout[...], NT).astype(BF16)

    def project(h):
        u_s[...] = dot(xn[...], win[h])

    def u_of(i):
        return u_s[ROWS * i : ROWS * (i + 1)]

    def exchange(i, total):
        esend[i] = total[pl.ds(other, HALF)].astype(BF16)
        copy = remote(esend.at[i], erecv.at[i], ex_send.at[i], ex_recv.at[i], (s, me, 1 - c))
        copy.start()
        sent.append(copy)
        return copy

    def ahead_end(t, copy):
        copy.wait_recv()
        out = (
            xsrc[t, pl.ds(mine, HALF)].astype(F32)
            + part[pl.ds(mine, HALF)]
            + erecv[t].astype(F32)
        )
        outs[0, t] = out.astype(BF16)

    def back_end(t, copy):
        copy.wait_recv()
        d = dxn[pl.ds(mine, HALF)] + erecv[2 + t].astype(F32)
        saved = stash[t, pl.ds(mine, HALF)].astype(F32)
        root = inverse_rms(saved)
        saved = saved * root
        back = root * (d - saved * jnp.mean(d * saved, axis=-1, keepdims=True))
        outs[1, t] = (gsrc[t, pl.ds(mine, HALF)].astype(F32) + back).astype(BF16)

    stores = []

    def store(i, t, ref):
        copy = pltpu.make_async_copy(outs.at[i, t], ref.at[0, t], st_sem.at[2 * i + t])
        copy.start()
        stores.append(copy)

    def relay(i, held, to):
        half = held.at[1, pl.ds(mine, HALF)]
        far = remote(outs.at[i, 0], half, sec_send.at[i], sec_recv.at[i], (to, me, c))
        far.start()
        sent.append(far)
        return far

    def hand_on(i, held, far):
        half = held.at[1, pl.ds(mine, HALF)]
        far.wait_recv()
        near = remote(half, half, fw_send.at[i], fw_recv.at[i], (s, me, 1 - c))
        near.start()
        sent.append(near)
        return near

    forward(0)
    spread(1)
    finish(0)
    project(0)
    ahead_later = []
    back_first(0, 0, u_of(1))
    back_first(1, 0, u_of(2))
    a_u0 = u_of(0)
    ahead_later.append(heads_forward(a_u0, keep_s[0])[0])

    forward(1)
    spread(2)
    begin(3)
    finish(1)
    project(1)
    back_first(0, 1, u_of(1))
    back_first(1, 1, u_of(2))
    ahead_later.append(heads_forward(u_of(0), keep_s[0])[0])

    forward(2)
    spread(3)
    begin(4)
    finish(2)
    part[...] = dot(jnp.concatenate(ahead_later, axis=1), wout[: 2 * HEAD, :])
    gated_grad(0)
    back_second(0, 0)
    back_second(0, 1)

    forward(3)
    spread(4)
    finish(3)
    project(2)
    ahead_part(0, 2, u_of(0))
    back_first(0, 2, u_of(1))
    back_first(1, 2, u_of(2))
    back_second(0, 2)

    forward(4)
    finish(4)
    project(3)
    ahead_part(0, 3, u_of(0))
    ahead_copy = exchange(0, part)
    back_first(0, 3, u_of(1))
    back_second(0, 3)
    back_copy = exchange(2, dxn)
    ahead_end(0, ahead_copy)
    ahead_far = relay(0, xin, ahead)
    store(0, 0, acts_out)
    back_end(0, back_copy)
    back_far = relay(1, gin, behind)
    store(1, 0, grads_out)

    back_first(1, 3, u_of(2))
    begin(5)
    a2a_start(0)
    spread(5)

    ahead_near = hand_on(0, xin, ahead_far)
    forward(5)
    ahead_near.wait_recv()
    xsrc[1] = jnp.where(s == 0, xsrc[1], xin[1])
    xn[0:ROWS] = normed(xsrc[1])
    for h in range(HEADS):
        ahead_part(1, h, dot(xn[0:ROWS], win[h]))
    ahead_copy = exchange(1, part)

    back_near = hand_on(1, gin, back_far)
    back_near.wait_recv()
    gsrc[1] = jnp.where(s == sections - 1, gsrc[1], gin[1])
    a2a_start(1)
    ahead_end(1, ahead_copy)
    store(0, 1, acts_out)
    gated_grad(1)
    for h in range(HEADS):
        back_second(1, h)
    back_copy = exchange(3, dxn)

    finish(5)
    a2a_wait(0)

    def weight_term(t):
        return dot(
            gcol[t].reshape(NDP * ROWS, SHARD), gat[t].reshape(NDP * ROWS, HEADS * HEAD), TN
        )

    total = weight_term(0)
    back_end(1, back_copy)
    store(1, 1, grads_out)
    a2a_wait(1)
    total = (total + weight_term(1)) * (TICKS * ROWS * NDP) ** -0.5
    wg_s[...] = total.T
    last = pltpu.make_async_copy(wg_s, wgrad_out.at[0], st_sem.at[4])
    last.start()
    for copy in sent + a2a_sent:
        copy.wait_send()
    for copy in stores + [last]:
        copy.wait()


def solution(mesh):
    sections = mesh.shape["section"]
    in_specs = (
        P(None, "dp", None),
        P("section", "dp", None),
        P(None, "dp", None),
        P("section", "dp", None),
        P("section", None, "dp", None),
        P("section", "dp", "cores"),
        P("section", "cores", "dp"),
        P("dp", None),
        P("dp", None),
        P("dp", None, None, None),
        P("dp", None, None, None),
    )
    out_specs = (
        P("section", None, ("dp", "cores"), None),
        P("section", None, ("dp", "cores"), None),
        P("section", "cores", "dp"),
    )
    dma, vmem = pltpu.SemaphoreType.DMA, pltpu.VMEM
    scratch = [
        vmem((HEADS, D, WIDE), BF16),
        vmem((HEADS * HEAD, D), BF16),
        vmem((TICKS, NDP, ROWS, HEADS * HEAD), BF16),
        vmem((TICKS, NDP, ROWS, SHARD), BF16),
        vmem((TICKS, ROWS, D), BF16),
        vmem((TICKS, ROWS, D), BF16),
        vmem((TICKS, ROWS, D), BF16),
        vmem((TICKS, ROWS, D), BF16),
        vmem((TICKS, ROWS, D), BF16),
        vmem((3 * ROWS, D), BF16),
        vmem((3 * ROWS, WIDE), F32),
        vmem((ROWS, D), F32),
        vmem((ROWS, D), F32),
        vmem((ROWS, HEADS * HEAD), BF16),
        vmem((TICKS, HEADS, ROWS, WIDE), F32),
        vmem((TICKS, HEADS, ROWS, HEAD), F32),
        vmem((TICKS, HEADS, ROWS, HEAD), F32),
        vmem((TICKS, HEADS, ROWS, HEAD), F32),
        vmem((TICKS, HEADS, ROWS, HEAD), BF16),
        vmem((TICKS, HEADS, ROWS, HEAD), BF16),
        vmem((TICKS, HEADS, ROWS, HEAD), BF16),
        vmem((TICKS, HEADS, ROWS, ROWS), BF16),
        vmem((TICKS, HEADS, ROWS, ROWS), F32),
        vmem((2 * TICKS, ROWS, ROWS), F32),
        vmem((2 * TICKS, HALF, D), BF16),
        vmem((2 * TICKS, HALF, D), BF16),
        vmem((2, TICKS, HALF, D), BF16),
        vmem((HEADS * HEAD, SHARD), F32),
        dma((10,)),
        dma((6, NDP)),
        dma((6, 15)),
        dma((4,)),
        dma((4,)),
        dma((2,)),
        dma((2,)),
        dma((2,)),
        dma((2,)),
        dma((TICKS, NDP)),
        dma((TICKS, NDP)),
        dma((5,)),
    ]

    def per_device(*args):
        any_spec = pl.BlockSpec(memory_space=pl.ANY)
        smem_spec = pl.BlockSpec(memory_space=pltpu.SMEM)

        def body(*refs):
            kernel(sections, *refs)

        return pl.pallas_call(
            body,
            out_shape=(
                jax.ShapeDtypeStruct((1, TICKS, HALF, D), BF16),
                jax.ShapeDtypeStruct((1, TICKS, HALF, D), BF16),
                jax.ShapeDtypeStruct((1, HEADS * HEAD, SHARD), F32),
            ),
            in_specs=[any_spec] * 7 + [smem_spec] * 4,
            out_specs=(any_spec,) * 3,
            scratch_shapes=scratch,
            compiler_params=pltpu.CompilerParams(
                collective_id=0, has_side_effects=True, vmem_limit_bytes=58 * 2**20
            ),
            name="window",
        )(*args)

    return jax.shard_map(
        per_device, mesh=mesh, in_specs=in_specs, out_specs=out_specs, check_vma=False
    )
```

```python
import jax
import jax.numpy as jnp
from jax import lax
from jax.experimental import pallas as pl
from jax.experimental.pallas import tpu as pltpu
from jax.sharding import PartitionSpec as P

HEAD = 128
HEADS = 4
WIDE = 4 * HEAD
BLOCK = 24
BLOCKS = 4
ROWS = BLOCK * BLOCKS
HALF = ROWS // 2
D = 2048
TICKS = 2
NZ, NX = 4, 4
NDP = NZ * NX
SHARD = D // NDP
EPSILON = 1e-06
SCALE = HEAD**-0.5
MESH = pl.DeviceIdType.MESH
F32, BF16 = jnp.float32, jnp.bfloat16

NT = (((1,), (1,)), ((), ()))
TN = (((0,), (0,)), ((), ()))


def sigmoid(v):
    return 1.0 / (1.0 + jnp.exp(-v))


def dot(a, b, dims=(((1,), (0,)), ((), ()))):
    return lax.dot_general(a, b, dims, preferred_element_type=F32)


def inverse_rms(v):
    return lax.rsqrt(jnp.mean(v * v, axis=-1, keepdims=True) + EPSILON)


def keep_count(blocks, marks, history):
    i = lax.broadcasted_iota(jnp.int32, (ROWS, ROWS), 0)
    j = lax.broadcasted_iota(jnp.int32, (ROWS, ROWS), 1)

    def owner(p):
        return sum((p >= BLOCK * b).astype(jnp.int32) for b in range(1, BLOCKS))

    bi, bj = owner(i), owner(j)
    spread = (bi == bj).astype(jnp.int32)
    for a in range(1, BLOCKS):
        for b in range(a):
            here = ((bi == a) & (bj == b)).astype(jnp.int32)
            spread = spread + here * marks[0, a, b, history]
    live = jnp.full((ROWS, ROWS), blocks[0, history] * BLOCK, jnp.int32)
    keep = (spread > 0) & (j <= i) & (i < live) & (j < live)
    return jnp.where(keep, 1.0 / live.astype(F32), 0.0)


def kernel(
    sections,
    arrivals,
    in_flight,
    cotangent,
    grad_flight,
    stashed,
    in_weight,
    out_weight,
    f_blocks,
    b_blocks,
    f_marks,
    b_marks,
    acts_out,
    grads_out,
    wgrad_out,
    win,
    wout,
    gat,
    gcol,
    xin,
    gin,
    xsrc,
    gsrc,
    stash,
    xn,
    u_s,
    part,
    dxn,
    dgat,
    dsil_s,
    gate_s,
    norm_s,
    rs_s,
    v_s,
    q_s,
    k_s,
    p_s,
    dsc_s,
    keep_s,
    esend,
    erecv,
    outs,
    wg_s,
    wsum,
    wsend,
    wrecv,
    load_sem,
    ag_recv,
    ag_send,
    ex_send,
    ex_recv,
    sec_send,
    sec_recv,
    fw_send,
    fw_recv,
    a2a_send,
    a2a_recv,
    w_send,
    w_recv,
    st_sem,
):
    s = lax.axis_index("section")
    me = lax.axis_index("dp")
    c = lax.axis_index("cores")
    z, x = me // NX, me % NX
    right, left, across = (x + 1) % NX, (x + NX - 1) % NX, (x + 2) % NX
    near_z = z - 1 + 2 * ((NZ - 1 - z) // (NZ - 1))
    far_z = (NZ - 1) * (1 - z // 2)
    peer_z = (near_z, 6 - z - near_z - far_z, far_z)
    zs = (z,) + peer_z
    inner = z % (NZ - 1) != 0
    hop_z = (z + 1, z - 1, (NZ - 1) * (z - 1))
    ahead, behind = (s + 1) % sections, (s + sections - 1) % sections
    mine, other = pl.multiple_of(c * HALF, 16), pl.multiple_of((1 - c) * HALF, 16)

    barrier = pltpu.get_barrier_semaphore()
    for k in range(1, NDP):
        pl.semaphore_signal(barrier, inc=1, device_id=(s, (me + k) % NDP, c), device_id_type=MESH)
    pl.semaphore_signal(barrier, inc=1, device_id=(s, me, 1 - c), device_id_type=MESH)
    pl.semaphore_signal(barrier, inc=1, device_id=(ahead, me, c), device_id_type=MESH)
    pl.semaphore_signal(barrier, inc=1, device_id=(behind, me, c), device_id_type=MESH)

    def chunk(n, owner):
        if n == HEADS:
            return wout.at[:, pl.ds(pl.multiple_of(owner * SHARD, SHARD), SHARD)]
        if n == HEADS + 1:
            return gat.at[:, owner % NX]
        return win.at[n, pl.ds(pl.multiple_of(owner * SHARD, SHARD), SHARD), :]

    loads = []
    for h in range(HEADS):
        loads.append((in_weight.at[0, :, pl.ds(h * WIDE, WIDE)], chunk(h, me)))
    loads.append((out_weight.at[0], chunk(HEADS, me)))
    loads += [
        (stashed.at[0], stash),
        (arrivals, xsrc),
        (in_flight.at[0], xin.at[0]),
        (cotangent, gsrc),
        (grad_flight.at[0], gin.at[0]),
    ]
    loads = [pltpu.make_async_copy(a, b, load_sem.at[i]) for i, (a, b) in enumerate(loads)]
    for copy in loads:
        copy.start()

    def remote(src, dst, send, recv, to):
        return pltpu.make_async_remote_copy(
            src_ref=src, dst_ref=dst, send_sem=send, recv_sem=recv, device_id=to, device_id_type=MESH
        )

    sent = []

    def start(copy, cond=None):
        if cond is None:
            copy.start()
        else:
            pl.when(cond)(copy.start)
        sent.append((copy, cond))

    def ag(n, owner, slot, to_z, to_x):
        block = chunk(n, owner)
        return remote(
            block, block, ag_send.at[n, slot], ag_recv.at[n, owner], (s, to_z * NX + to_x, c)
        )

    def push(n, owner, slot, to_z, to_x, cond=None):
        start(ag(n, owner, slot, to_z, to_x), cond)

    def arrive(n, owner):
        ag(n, owner, 0, z, right).wait_recv()

    def begin(n):
        push(n, me, 0, z, right)
        push(n, me, 1, z, left)
        push(n, me, 2, z + 1, x, z < NZ - 1)
        push(n, me, 3, z - 1, x, z > 0)

    def spread(n):
        for i in range(3):
            owner = peer_z[i] * NX + x
            arrive(n, owner)
            push(n, owner, 10 + i, hop_z[i], x, inner)
            push(n, owner, 4 + 2 * i, z, right)
            push(n, owner, 5 + 2 * i, z, left)

    def forward(n):
        for i in range(4):
            from_left, from_right = zs[i] * NX + left, zs[i] * NX + right
            if i in (0, 3):
                arrive(n, from_left)
                push(n, from_left, 13 + i, z, right)
                arrive(n, from_right)
            else:
                arrive(n, from_right)
                push(n, from_right, 13 + i, z, left)
                arrive(n, from_left)

    def finish(n):
        for i in range(4):
            arrive(n, zs[i] * NX + across)

    xs = (x, right, left, across)
    OUT, GATED = HEADS, HEADS + 1

    def ring(n):
        for i in range(1, NX):
            push(n, me, i - 1, z, xs[i])

    def line(i):
        owner = z * NX + xs[i]
        if i:
            arrive(OUT, owner)
        for k in range(3):
            push(OUT, owner, 3 + 3 * i + k, peer_z[k], xs[0])

    def finish_line():
        for i in range(NX):
            for k in range(3):
                arrive(OUT, peer_z[k] * NX + xs[i])

    def finish_ring():
        for i in range(1, NX):
            arrive(GATED, z * NX + xs[i])

    loads[0].wait()
    pl.semaphore_wait(barrier, NDP - 1 + 3)
    begin(0)
    loads[HEADS].wait()
    ring(OUT)
    loads[1].wait()
    begin(1)

    for t in range(TICKS):
        keep_s[t] = keep_count(f_blocks, f_marks, t - s + sections - 1)
        keep_s[2 + t] = keep_count(b_blocks, b_marks, t + s)

    def normed(v):
        v = v.astype(F32)
        return (v * inverse_rms(v)).astype(BF16)

    spread(0)
    line(0)
    for copy in loads[2:HEADS] + loads[HEADS + 1 :]:
        copy.wait()

    xsrc[0] = jnp.where(s == 0, xsrc[0], xin[0])
    gsrc[0] = jnp.where(s == sections - 1, gsrc[0], gin[0])
    xn[0:ROWS] = normed(xsrc[0])
    for t in range(TICKS):
        xn[ROWS * (t + 1) : ROWS * (t + 2)] = normed(stash[t])

    def columns(owner_z, owner_x):
        return pl.ds(pl.multiple_of((owner_z * NX + owner_x) * SHARD, SHARD), SHARD)

    def a2a(t, i, owner_z, sender):
        return remote(
            gsrc.at[t, :, columns(owner_z, xs[i])],
            gcol.at[t, sender, :, pl.ds(owner_z * SHARD, SHARD)],
            a2a_send.at[t, i, owner_z],
            a2a_recv.at[t, sender, owner_z],
            (s, z * NX + xs[i], c),
        )

    def a2a_start(t):
        for owner_z in range(NZ):
            for i in range(1, NX):
                start(a2a(t, i, owner_z, x))
            gcol[t, x, :, owner_z * SHARD : (owner_z + 1) * SHARD] = gsrc[t, :, columns(owner_z, x)]

    def a2a_wait(t):
        for owner_z in range(NZ):
            for i in range(1, NX):
                a2a(t, i, owner_z, xs[i]).wait_recv()

    def heads_forward(u, keep):
        sg = sigmoid(u)
        act = u * sg
        gate = act[:, :HEAD]
        v = act[:, HEAD : 2 * HEAD].astype(BF16)
        q = act[:, 2 * HEAD : 3 * HEAD].astype(BF16)
        k = act[:, 3 * HEAD :].astype(BF16)
        scores = dot(q, k, NT) * SCALE
        ss = sigmoid(scores)
        probs = (scores * ss * keep).astype(BF16)
        mixed = dot(probs, v)
        rs = inverse_rms(mixed)
        norm = mixed * rs
        return (norm * gate).astype(BF16), (sg, gate, v, q, k, scores, ss, probs, rs, norm)

    def ahead_part(t, h, u):
        gated, _ = heads_forward(u, keep_s[t])
        more = dot(gated, wout[h * HEAD : (h + 1) * HEAD, :])
        if h == 0:
            part[...] = more
        else:
            part[...] += more

    def back_first(t, h, u):
        keep = keep_s[2 + t]
        gated, (sg, gate, v, q, k, scores, ss, probs, rs, norm) = heads_forward(u, keep)
        gat[t, x, :, h * HEAD : (h + 1) * HEAD] = gated
        dsil_s[t, h] = sg * (1.0 + u * (1.0 - sg))
        gate_s[t, h] = gate
        norm_s[t, h] = norm
        rs_s[t, h] = jnp.broadcast_to(rs, (ROWS, HEAD))
        v_s[t, h] = v
        q_s[t, h] = q
        k_s[t, h] = k
        p_s[t, h] = probs
        dsc_s[t, h] = keep * ss * (1.0 + scores * (1.0 - ss)) * SCALE

    def back_second(t, h):
        dg = dgat[:, h * HEAD : (h + 1) * HEAD].astype(F32)
        norm = norm_s[t, h]
        dn = dg * gate_s[t, h]
        dgate = dg * norm
        dm = (rs_s[t, h] * (dn - norm * jnp.mean(dn * norm, axis=-1, keepdims=True))).astype(BF16)
        dp = dot(dm, v_s[t, h], NT)
        dv = dot(p_s[t, h], dm, TN)
        ds = (dp * dsc_s[t, h]).astype(BF16)
        dq = dot(ds, k_s[t, h])
        dk = dot(ds, q_s[t, h], TN)
        du = (jnp.concatenate([dgate, dv, dq, dk], axis=1) * dsil_s[t, h]).astype(BF16)
        more = dot(du, win[h], NT)
        if h == 0:
            dxn[...] = more
        else:
            dxn[...] += more

    def gated_grad(t):
        dgat[...] = dot(gsrc[t], wout[...], NT).astype(BF16)

    def project(h):
        u_s[...] = dot(xn[...], win[h])

    def u_of(i):
        return u_s[ROWS * i : ROWS * (i + 1)]

    def exchange(i, total):
        esend[i] = total[pl.ds(other, HALF)].astype(BF16)
        copy = remote(esend.at[i], erecv.at[i], ex_send.at[i], ex_recv.at[i], (s, me, 1 - c))
        start(copy)
        return copy

    def ahead_end(t, copy):
        copy.wait_recv()
        out = (
            xsrc[t, pl.ds(mine, HALF)].astype(F32)
            + part[pl.ds(mine, HALF)]
            + erecv[t].astype(F32)
        )
        outs[0, t] = out.astype(BF16)

    def back_end(t, copy):
        copy.wait_recv()
        d = dxn[pl.ds(mine, HALF)] + erecv[2 + t].astype(F32)
        saved = stash[t, pl.ds(mine, HALF)].astype(F32)
        root = inverse_rms(saved)
        saved = saved * root
        back = root * (d - saved * jnp.mean(d * saved, axis=-1, keepdims=True))
        outs[1, t] = (gsrc[t, pl.ds(mine, HALF)].astype(F32) + back).astype(BF16)

    stores = []

    def store(i, t, ref):
        copy = pltpu.make_async_copy(outs.at[i, t], ref.at[0, t], st_sem.at[2 * i + t])
        copy.start()
        stores.append(copy)

    def relay(i, held, to):
        half = held.at[1, pl.ds(mine, HALF)]
        far = remote(outs.at[i, 0], half, sec_send.at[i], sec_recv.at[i], (to, me, c))
        start(far)
        return far

    def hand_on(i, held, far):
        half = held.at[1, pl.ds(mine, HALF)]
        far.wait_recv()
        near = remote(half, half, fw_send.at[i], fw_recv.at[i], (s, me, 1 - c))
        start(near)
        return near

    gated_ahead = []

    def first(h):
        project(h)
        for t in range(TICKS):
            back_first(t, h, u_of(1 + t))
        gated_ahead.append(heads_forward(u_of(0), keep_s[0])[0])

    forward(0)
    spread(1)
    begin(2)
    line(1)
    finish(0)
    first(0)

    forward(1)
    spread(2)
    begin(3)
    line(2)
    finish(1)
    first(1)

    forward(2)
    spread(3)
    line(3)
    finish(2)
    first(2)

    forward(3)
    finish_line()
    part[...] = dot(jnp.concatenate(gated_ahead, axis=1), wout[: 3 * HEAD, :])
    gated_grad(0)
    for h in range(3):
        back_second(0, h)

    finish(3)
    project(3)
    back_first(0, 3, u_of(1))
    back_second(0, 3)
    back_copy = exchange(2, dxn)
    ahead_part(0, 3, u_of(0))
    ahead_copy = exchange(0, part)
    back_end(0, back_copy)
    back_far = relay(1, gin, behind)
    store(1, 0, grads_out)
    ahead_end(0, ahead_copy)
    ahead_far = relay(0, xin, ahead)
    store(0, 0, acts_out)

    back_first(1, 3, u_of(2))
    ring(GATED)
    a2a_start(0)
    finish_ring()
    a2a_wait(0)

    def weight_term(t):
        return dot(gat[t].reshape(NX * ROWS, HEADS * HEAD), gcol[t].reshape(NX * ROWS, NZ * SHARD), TN)

    wsum[...] = weight_term(0)

    back_near = hand_on(1, gin, back_far)
    back_near.wait_recv()
    gsrc[1] = jnp.where(s == sections - 1, gsrc[1], gin[1])
    a2a_start(1)
    gated_grad(1)
    back_second(1, 0)
    back_second(1, 1)

    a2a_wait(1)
    wsum[...] += weight_term(1)

    def wblock(owner_z):
        return wsum[:, pl.ds(pl.multiple_of(owner_z * SHARD, SHARD), SHARD)]

    def wcopy(i, sender):
        return remote(
            wsend.at[i], wrecv.at[sender], w_send.at[i], w_recv.at[sender], (s, peer_z[i] * NX + x, c)
        )

    for i in range(3):
        wsend[i] = wblock(peer_z[i]).astype(BF16)
        start(wcopy(i, z))

    back_second(1, 2)
    back_second(1, 3)
    back_copy = exchange(3, dxn)

    ahead_near = hand_on(0, xin, ahead_far)
    ahead_near.wait_recv()
    xsrc[1] = jnp.where(s == 0, xsrc[1], xin[1])
    xn[0:ROWS] = normed(xsrc[1])
    for h in range(HEADS):
        ahead_part(1, h, dot(xn[0:ROWS], win[h]))
    ahead_copy = exchange(1, part)
    back_end(1, back_copy)
    store(1, 1, grads_out)
    ahead_end(1, ahead_copy)
    store(0, 1, acts_out)

    total = wblock(z)
    for i in range(3):
        wcopy(i, peer_z[i]).wait_recv()
        total = total + wrecv[peer_z[i]].astype(F32)
    wg_s[...] = total * (TICKS * ROWS * NDP) ** -0.5
    last = pltpu.make_async_copy(wg_s, wgrad_out.at[0], st_sem.at[4])
    last.start()
    for copy, cond in sent:
        if cond is None:
            copy.wait_send()
        else:
            pl.when(cond)(copy.wait_send)
    for copy in stores + [last]:
        copy.wait()


def solution(mesh):
    sections = mesh.shape["section"]
    in_specs = (
        P(None, "dp", None),
        P("section", "dp", None),
        P(None, "dp", None),
        P("section", "dp", None),
        P("section", None, "dp", None),
        P("section", "dp", "cores"),
        P("section", "cores", "dp"),
        P("dp", None),
        P("dp", None),
        P("dp", None, None, None),
        P("dp", None, None, None),
    )
    out_specs = (
        P("section", None, ("dp", "cores"), None),
        P("section", None, ("dp", "cores"), None),
        P("section", "cores", "dp"),
    )
    dma, vmem = pltpu.SemaphoreType.DMA, pltpu.VMEM
    scratch = [
        vmem((HEADS, D, WIDE), BF16),
        vmem((HEADS * HEAD, D), BF16),
        vmem((TICKS, NX, ROWS, HEADS * HEAD), BF16),
        vmem((TICKS, NX, ROWS, NZ * SHARD), BF16),
        vmem((TICKS, ROWS, D), BF16),
        vmem((TICKS, ROWS, D), BF16),
        vmem((TICKS, ROWS, D), BF16),
        vmem((TICKS, ROWS, D), BF16),
        vmem((TICKS, ROWS, D), BF16),
        vmem((3 * ROWS, D), BF16),
        vmem((3 * ROWS, WIDE), F32),
        vmem((ROWS, D), F32),
        vmem((ROWS, D), F32),
        vmem((ROWS, HEADS * HEAD), BF16),
        vmem((TICKS, HEADS, ROWS, WIDE), F32),
        vmem((TICKS, HEADS, ROWS, HEAD), F32),
        vmem((TICKS, HEADS, ROWS, HEAD), F32),
        vmem((TICKS, HEADS, ROWS, HEAD), F32),
        vmem((TICKS, HEADS, ROWS, HEAD), BF16),
        vmem((TICKS, HEADS, ROWS, HEAD), BF16),
        vmem((TICKS, HEADS, ROWS, HEAD), BF16),
        vmem((TICKS, HEADS, ROWS, ROWS), BF16),
        vmem((TICKS, HEADS, ROWS, ROWS), F32),
        vmem((2 * TICKS, ROWS, ROWS), F32),
        vmem((2 * TICKS, HALF, D), BF16),
        vmem((2 * TICKS, HALF, D), BF16),
        vmem((2, TICKS, HALF, D), BF16),
        vmem((HEADS * HEAD, SHARD), F32),
        vmem((HEADS * HEAD, NZ * SHARD), F32),
        vmem((3, HEADS * HEAD, SHARD), BF16),
        vmem((NZ, HEADS * HEAD, SHARD), BF16),
        dma((10,)),
        dma((6, NDP)),
        dma((6, 17)),
        dma((4,)),
        dma((4,)),
        dma((2,)),
        dma((2,)),
        dma((2,)),
        dma((2,)),
        dma((TICKS, NX, NZ)),
        dma((TICKS, NX, NZ)),
        dma((3,)),
        dma((NZ,)),
        dma((5,)),
    ]

    def per_device(*args):
        marks = [jnp.transpose(m, (0, 2, 3, 1)) for m in args[9:]]
        any_spec = pl.BlockSpec(memory_space=pl.ANY)
        smem_spec = pl.BlockSpec(memory_space=pltpu.SMEM)

        def body(*refs):
            kernel(sections, *refs)

        return pl.pallas_call(
            body,
            out_shape=(
                jax.ShapeDtypeStruct((1, TICKS, HALF, D), BF16),
                jax.ShapeDtypeStruct((1, TICKS, HALF, D), BF16),
                jax.ShapeDtypeStruct((1, HEADS * HEAD, SHARD), F32),
            ),
            in_specs=[any_spec] * 7 + [smem_spec] * 4,
            out_specs=(any_spec,) * 3,
            scratch_shapes=scratch,
            compiler_params=pltpu.CompilerParams(
                collective_id=0, has_side_effects=True, vmem_limit_bytes=58 * 2**20
            ),
            name="window",
        )(*args[:9], *marks)

    return jax.shard_map(
        per_device, mesh=mesh, in_specs=in_specs, out_specs=out_specs, check_vma=False
    )
```

```python
import jax
import jax.numpy as jnp
from jax import lax
from jax.experimental import pallas as pl
from jax.experimental.pallas import tpu as pltpu
from jax.sharding import PartitionSpec as P

HEAD = 128
AHEAD_AFTER = 2
HEADS = 4
WIDE = 4 * HEAD
BLOCK = 24
BLOCKS = 4
ROWS = BLOCK * BLOCKS
HALF = ROWS // 2
D = 2048
TICKS = 2
NZ, NX = 4, 4
NDP = NZ * NX
PARTS = D // WIDE
SHARD = D // NDP
EPSILON = 1e-06
SCALE = HEAD**-0.5
MESH = pl.DeviceIdType.MESH
F32, BF16 = jnp.float32, jnp.bfloat16

NT = (((1,), (1,)), ((), ()))
TN = (((0,), (0,)), ((), ()))


def sigmoid(v):
    return 1.0 / (1.0 + jnp.exp(-v))


def dot(a, b, dims=(((1,), (0,)), ((), ()))):
    return lax.dot_general(a, b, dims, preferred_element_type=F32)


def inverse_rms(v):
    return lax.rsqrt(jnp.mean(v * v, axis=-1, keepdims=True) + EPSILON)


def keep_count(blocks, marks, history):
    i = lax.broadcasted_iota(jnp.int32, (ROWS, ROWS), 0)
    j = lax.broadcasted_iota(jnp.int32, (ROWS, ROWS), 1)

    def owner(p):
        return sum((p >= BLOCK * b).astype(jnp.int32) for b in range(1, BLOCKS))

    bi, bj = owner(i), owner(j)
    spread = (bi == bj).astype(jnp.int32)
    for a in range(1, BLOCKS):
        for b in range(a):
            here = ((bi == a) & (bj == b)).astype(jnp.int32)
            spread = spread + here * marks[0, a, b, history]
    live = jnp.full((ROWS, ROWS), blocks[0, history] * BLOCK, jnp.int32)
    keep = (spread > 0) & (j <= i) & (i < live) & (j < live)
    return jnp.where(keep, 1.0 / live.astype(F32), 0.0)


def kernel(
    sections,
    arrivals,
    in_flight,
    cotangent,
    grad_flight,
    stashed,
    in_weight,
    out_weight,
    f_blocks,
    b_blocks,
    f_marks,
    b_marks,
    acts_out,
    grads_out,
    wgrad_out,
    win,
    wout,
    gat,
    gcol,
    xin,
    gin,
    xsrc,
    gsrc,
    stash,
    xn,
    u_s,
    part,
    dxn,
    dgat,
    dgat_s,
    u_next,
    dsil_s,
    gate_s,
    norm_s,
    rs_s,
    v_s,
    q_s,
    k_s,
    p_s,
    dsc_s,
    keep_s,
    esend,
    erecv,
    outs,
    wg_s,
    wsum,
    wsend,
    wrecv,
    load_sem,
    ag_recv,
    ag_send,
    ex_send,
    ex_recv,
    sec_send,
    sec_recv,
    fw_send,
    fw_recv,
    a2a_send,
    a2a_recv,
    pair_send,
    pair_recv,
    w_send,
    w_recv,
    st_sem,
):
    s = lax.axis_index("section")
    me = lax.axis_index("dp")
    c = lax.axis_index("cores")
    z, x = me // NX, me % NX
    right, left, across = (x + 1) % NX, (x + NX - 1) % NX, (x + 2) % NX
    near_z = z - 1 + 2 * ((NZ - 1 - z) // (NZ - 1))
    far_z = (NZ - 1) * (1 - z // 2)
    peer_z = (near_z, 6 - z - near_z - far_z, far_z)
    zs = (z,) + peer_z
    inner = z % (NZ - 1) != 0
    hop_z = (z + 1, z - 1, (NZ - 1) * (z - 1))
    ahead, behind = (s + 1) % sections, (s + sections - 1) % sections
    mine, other = pl.multiple_of(c * HALF, 16), pl.multiple_of((1 - c) * HALF, 16)

    barrier = pltpu.get_barrier_semaphore()
    for k in range(1, NDP):
        pl.semaphore_signal(barrier, inc=1, device_id=(s, (me + k) % NDP, c), device_id_type=MESH)
    pl.semaphore_signal(barrier, inc=1, device_id=(s, me, 1 - c), device_id_type=MESH)
    pl.semaphore_signal(barrier, inc=1, device_id=(ahead, me, c), device_id_type=MESH)
    pl.semaphore_signal(barrier, inc=1, device_id=(behind, me, c), device_id_type=MESH)

    def chunk(n, owner):
        if n == HEADS:
            return wout.at[:, pl.ds(pl.multiple_of(owner * SHARD, SHARD), SHARD)]
        if n == HEADS + 1:
            return gat.at[0, owner % NX]
        if n == HEADS + 2:
            return gat.at[1, owner % NX]
        return win.at[n, pl.ds(pl.multiple_of(owner * SHARD, SHARD), SHARD), :]

    loads = []
    for h in range(HEADS):
        loads.append((in_weight.at[0, :, pl.ds(h * WIDE, WIDE)], chunk(h, me)))
    loads.append((out_weight.at[0], chunk(HEADS, me)))
    loads += [
        (stashed.at[0], stash),
        (arrivals, xsrc),
        (in_flight.at[0], xin.at[0]),
        (cotangent, gsrc),
        (grad_flight.at[0], gin.at[0]),
    ]
    loads = [pltpu.make_async_copy(a, b, load_sem.at[i]) for i, (a, b) in enumerate(loads)]
    for copy in loads:
        copy.start()

    def remote(src, dst, send, recv, to):
        return pltpu.make_async_remote_copy(
            src_ref=src, dst_ref=dst, send_sem=send, recv_sem=recv, device_id=to, device_id_type=MESH
        )

    sent = []

    def start(copy, cond=None):
        if cond is None:
            copy.start()
        else:
            pl.when(cond)(copy.start)
        sent.append((copy, cond))

    def ag(n, owner, slot, to_z, to_x):
        block = chunk(n, owner)
        return remote(
            block, block, ag_send.at[n, slot], ag_recv.at[n, owner], (s, to_z * NX + to_x, c)
        )

    def push(n, owner, slot, to_z, to_x, cond=None):
        start(ag(n, owner, slot, to_z, to_x), cond)

    def arrive(n, owner):
        ag(n, owner, 0, z, right).wait_recv()

    def begin(n):
        push(n, me, 0, z, right)
        push(n, me, 1, z, left)
        push(n, me, 2, z + 1, x, z < NZ - 1)
        push(n, me, 3, z - 1, x, z > 0)

    def spread(n):
        for i in range(3):
            owner = peer_z[i] * NX + x
            arrive(n, owner)
            push(n, owner, 10 + i, hop_z[i], x, inner)
            push(n, owner, 4 + 2 * i, z, right)
            push(n, owner, 5 + 2 * i, z, left)

    def forward(n):
        for i in range(4):
            from_left, from_right = zs[i] * NX + left, zs[i] * NX + right
            if i in (0, 3):
                arrive(n, from_left)
                push(n, from_left, 13 + i, z, right)
                arrive(n, from_right)
            else:
                arrive(n, from_right)
                push(n, from_right, 13 + i, z, left)
                arrive(n, from_left)

    def finish(n):
        for i in range(4):
            arrive(n, zs[i] * NX + across)

    xs = (x, right, left, across)
    OUT, GATED = HEADS, HEADS + 1

    def ring(n):
        for i in range(1, NX):
            push(n, me, i - 1, z, xs[i])

    def ring_both():
        for t in range(TICKS):
            push(GATED + t, me, 0, z, right)
            push(GATED + t, me, 1, z, left)

    def pass_ring():
        for t in range(TICKS):
            arrive(GATED + t, z * NX + (left, right)[t])
            push(GATED + t, z * NX + (left, right)[t], 2, z, (right, left)[t])

    def line(i):
        owner = z * NX + xs[i]
        if i:
            arrive(OUT, owner)
        for k in range(3):
            push(OUT, owner, 3 + 3 * i + k, peer_z[k], xs[0])

    def finish_line():
        for i in range(NX):
            for k in range(3):
                arrive(OUT, peer_z[k] * NX + xs[i])

    def finish_ring():
        for t in range(TICKS):
            arrive(GATED + t, z * NX + (right, left)[t])
            arrive(GATED + t, z * NX + across)

    loads[0].wait()
    pl.semaphore_wait(barrier, NDP - 1 + 3)
    begin(0)
    loads[HEADS].wait()
    ring(OUT)
    loads[1].wait()
    begin(1)

    for t in range(TICKS):
        keep_s[t] = keep_count(f_blocks, f_marks, t - s + sections - 1)
        keep_s[2 + t] = keep_count(b_blocks, b_marks, t + s)

    def normed(v):
        v = v.astype(F32)
        return (v * inverse_rms(v)).astype(BF16)

    spread(0)
    line(0)
    for copy in loads[2:HEADS] + loads[HEADS + 1 :]:
        copy.wait()

    xsrc[0] = jnp.where(s == 0, xsrc[0], xin[0])
    gsrc[0] = jnp.where(s == sections - 1, gsrc[0], gin[0])
    xn[0:ROWS] = normed(xsrc[0])
    for t in range(TICKS):
        xn[ROWS * (t + 1) : ROWS * (t + 2)] = normed(stash[t])

    def columns(owner_z, owner_x):
        return pl.ds(pl.multiple_of((owner_z * NX + owner_x) * SHARD, SHARD), SHARD)

    def a2a(t, i, owner_z, sender):
        return remote(
            gsrc.at[t, pl.ds(mine, HALF), columns(owner_z, xs[i])],
            gcol.at[t, sender, pl.ds(mine, HALF), pl.ds(owner_z * SHARD, SHARD)],
            a2a_send.at[t, i, owner_z],
            a2a_recv.at[t, sender, owner_z],
            (s, z * NX + xs[i], c),
        )

    def a2a_start(t, *only):
        for owner_z in only or range(NZ):
            for i in range(1, NX):
                start(a2a(t, i, owner_z, x))

    def pair(t, i):
        half = gcol.at[t, xs[i], pl.ds(mine, HALF)]
        return remote(half, half, pair_send.at[t, i], pair_recv.at[t, i], (s, me, 1 - c))

    def a2a_pass(t):
        for i in range(1, NX):
            for owner_z in range(NZ):
                a2a(t, i, owner_z, xs[i]).wait_recv()
            start(pair(t, i))
        for owner_z in range(NZ):
            gcol[t, x, :, owner_z * SHARD : (owner_z + 1) * SHARD] = gsrc[t, :, columns(owner_z, x)]

    def a2a_wait(t):
        for i in range(1, NX):
            pair(t, i).wait_recv()

    def heads_forward(u, keep):
        sg = sigmoid(u)
        act = u * sg
        gate = act[:, :HEAD]
        v = act[:, HEAD : 2 * HEAD].astype(BF16)
        q = act[:, 2 * HEAD : 3 * HEAD].astype(BF16)
        k = act[:, 3 * HEAD :].astype(BF16)
        scores = dot(q, k, NT) * SCALE
        ss = sigmoid(scores)
        probs = (scores * ss * keep).astype(BF16)
        mixed = dot(probs, v)
        rs = inverse_rms(mixed)
        norm = mixed * rs
        return (norm * gate).astype(BF16), (sg, gate, v, q, k, scores, ss, probs, rs, norm)

    def ahead_part(t, h, u):
        gated, _ = heads_forward(u, keep_s[t])
        more = dot(gated, wout[h * HEAD : (h + 1) * HEAD, :])
        if h == 0:
            part[...] = more
        else:
            part[...] += more

    def back_first(t, h, u):
        keep = keep_s[2 + t]
        gated, (sg, gate, v, q, k, scores, ss, probs, rs, norm) = heads_forward(u, keep)
        gat[t, x, :, h * HEAD : (h + 1) * HEAD] = gated
        dsil_s[t, h] = sg * (1.0 + u * (1.0 - sg))
        gate_s[t, h] = gate
        norm_s[t, h] = norm
        rs_s[t, h] = jnp.broadcast_to(rs, (ROWS, HEAD))
        v_s[t, h] = v
        q_s[t, h] = q
        k_s[t, h] = k
        p_s[t, h] = probs
        dsc_s[t, h] = keep * ss * (1.0 + scores * (1.0 - ss)) * SCALE

    def back_second(t, h):
        dg = dgat[:, h * HEAD : (h + 1) * HEAD].astype(F32)
        norm = norm_s[t, h]
        dn = dg * gate_s[t, h]
        dgate = dg * norm
        dm = (rs_s[t, h] * (dn - norm * jnp.mean(dn * norm, axis=-1, keepdims=True))).astype(BF16)
        dp = dot(dm, v_s[t, h], NT)
        dv = dot(p_s[t, h], dm, TN)
        ds = (dp * dsc_s[t, h]).astype(BF16)
        dq = dot(ds, k_s[t, h])
        dk = dot(ds, q_s[t, h], TN)
        du = (jnp.concatenate([dgate, dv, dq, dk], axis=1) * dsil_s[t, h]).astype(BF16)
        more = dot(du, win[h], NT)
        if h == 0:
            dxn[...] = more
        else:
            dxn[...] += more

    def gated_grad(t):
        dgat[...] = dot(gsrc[t], wout[...], NT).astype(BF16)

    def project(h):
        u_s[...] = dot(xn[...], win[h])

    def u_of(i):
        return u_s[ROWS * i : ROWS * (i + 1)]

    def exchange(i, total):
        esend[i] = total[pl.ds(other, HALF)].astype(BF16)
        copy = remote(esend.at[i], erecv.at[i], ex_send.at[i], ex_recv.at[i], (s, me, 1 - c))
        start(copy)
        return copy

    def ahead_end(t, copy):
        copy.wait_recv()
        out = (
            xsrc[t, pl.ds(mine, HALF)].astype(F32)
            + part[pl.ds(mine, HALF)]
            + erecv[t].astype(F32)
        )
        outs[0, t] = out.astype(BF16)

    def back_end(t, copy):
        copy.wait_recv()
        d = dxn[pl.ds(mine, HALF)] + erecv[2 + t].astype(F32)
        saved = stash[t, pl.ds(mine, HALF)].astype(F32)
        root = inverse_rms(saved)
        saved = saved * root
        back = root * (d - saved * jnp.mean(d * saved, axis=-1, keepdims=True))
        outs[1, t] = (gsrc[t, pl.ds(mine, HALF)].astype(F32) + back).astype(BF16)

    stores = []

    def store(i, t, ref):
        copy = pltpu.make_async_copy(outs.at[i, t], ref.at[0, t], st_sem.at[2 * i + t])
        copy.start()
        stores.append(copy)

    def quarter(n):
        return slice(n * WIDE, (n + 1) * WIDE)

    def relay(i, held, to):
        copies = []
        for n in range(PARTS):
            half = held.at[1, pl.ds(mine, HALF), quarter(n)]
            copy = remote(
                outs.at[i, 0, :, quarter(n)], half, sec_send.at[i, n], sec_recv.at[i, n], (to, me, c)
            )
            start(copy)
            copies.append(copy)
        return copies

    def hand_on(i, n, held, far):
        half = held.at[1, pl.ds(mine, HALF), quarter(n)]
        far[n].wait_recv()
        near = remote(half, half, fw_send.at[i, n], fw_recv.at[i, n], (s, me, 1 - c))
        start(near)
        return near

    def drain():
        for copy, cond in sent:
            if cond is None:
                copy.wait_send()
            else:
                pl.when(cond)(copy.wait_send)
        sent.clear()

    gated_ahead = []

    def first(h):
        project(h)
        for t in range(TICKS):
            back_first(t, h, u_of(1 + t))
        gated_ahead.append(heads_forward(u_of(0), keep_s[0])[0])

    forward(0)
    spread(1)
    begin(2)
    line(1)
    finish(0)
    first(0)

    forward(1)
    spread(2)
    begin(3)
    line(2)
    finish(1)
    first(1)

    forward(2)
    spread(3)
    line(3)
    finish(2)
    first(2)

    forward(3)
    finish_line()
    part[...] = dot(jnp.concatenate(gated_ahead, axis=1), wout[: 3 * HEAD, :])
    gated_grad(0)
    for h in range(3):
        back_second(0, h)

    for i in range(NZ):
        arrive(3, zs[i] * NX + across)
        rows = pl.ds(pl.multiple_of(zs[i] * WIDE, WIDE), WIDE)
        more = dot(xn[:, rows], win[3, rows, :])
        if i == 0:
            u_s[...] = more
        else:
            u_s[...] += more
    back_first(0, 3, u_of(1))
    back_second(0, 3)
    back_copy = exchange(2, dxn)
    ahead_part(0, 3, u_of(0))
    ahead_copy = exchange(0, part)
    drained = sent[:-2]
    del sent[:-2]
    back_end(0, back_copy)
    back_far = relay(1, gin, behind)
    store(1, 0, grads_out)
    ahead_end(0, ahead_copy)
    store(0, 0, acts_out)

    back_first(1, 3, u_of(2))
    ring_both()
    a2a_start(0)
    held_back = sent[:]
    sent[:] = drained
    drain()
    sent[:] = held_back

    def weight_term(t):
        return dot(gat[t].reshape(NX * ROWS, HEADS * HEAD), gcol[t].reshape(NX * ROWS, NZ * SHARD), TN)

    def back_quarter(n, near):
        near.wait_recv()
        gsrc[1, pl.ds(other, HALF), quarter(n)] = jnp.where(
            s == sections - 1,
            gsrc[1, pl.ds(other, HALF), quarter(n)],
            gin[1, pl.ds(other, HALF), quarter(n)],
        )
        more = dot(gsrc[1, :, quarter(n)], wout[:, quarter(n)], NT)
        if n == 0:
            dgat_s[...] = more
        else:
            dgat_s[...] += more

    def ahead_quarter(n, near):
        near.wait_recv()
        rows = jnp.where(s == 0, xsrc[1, :, quarter(n)], xin[1, :, quarter(n)])
        xsrc[1, :, quarter(n)] = rows
        for h in range(HEADS):
            more = dot(rows, win[h, quarter(n), :])
            if n == 0:
                u_next[h] = more
            else:
                u_next[h] += more

    nears = []
    for n in range(PARTS):
        nears.append(hand_on(1, n, gin, back_far))
        gsrc[1, pl.ds(mine, HALF), quarter(n)] = jnp.where(
            s == sections - 1,
            gsrc[1, pl.ds(mine, HALF), quarter(n)],
            gin[1, pl.ds(mine, HALF), quarter(n)],
        )
        a2a_start(1, n)
        if n == 1:
            pass_ring()
        if n == 2:
            a2a_pass(0)
        if n == AHEAD_AFTER:
            ahead_far = relay(0, xin, ahead)
        if n:
            back_quarter(n - 1, nears[n - 1])
    back_quarter(PARTS - 1, nears[-1])
    a2a_pass(1)
    dgat[...] = dgat_s[...].astype(BF16)
    back_second(1, 0)
    back_second(1, 1)

    finish_ring()
    a2a_wait(0)
    wsum[...] = weight_term(0)
    a2a_wait(1)
    wsum[...] += weight_term(1)

    def wblock(owner_z):
        return wsum[:, pl.ds(pl.multiple_of(owner_z * SHARD, SHARD), SHARD)]

    def wcopy(i, sender):
        return remote(
            wsend.at[i], wrecv.at[sender], w_send.at[i], w_recv.at[sender], (s, peer_z[i] * NX + x, c)
        )

    for i in range(3):
        wsend[i] = wblock(peer_z[i]).astype(BF16)
        start(wcopy(i, z))

    nears = [hand_on(0, 0, xin, ahead_far)]
    back_second(1, 2)
    nears.append(hand_on(0, 1, xin, ahead_far))
    back_second(1, 3)
    back_copy = exchange(3, dxn)
    ahead_quarter(0, nears[0])
    nears.append(hand_on(0, 2, xin, ahead_far))
    ahead_quarter(1, nears[1])
    nears.append(hand_on(0, 3, xin, ahead_far))
    ahead_quarter(2, nears[2])
    back_end(1, back_copy)
    store(1, 1, grads_out)
    ahead_quarter(3, nears[3])
    root = inverse_rms(xsrc[1].astype(F32))
    gated = [heads_forward(u_next[h] * root, keep_s[1])[0] for h in range(HEADS)]
    part[...] = dot(jnp.concatenate(gated, axis=1), wout[...])
    ahead_copy = exchange(1, part)
    ahead_end(1, ahead_copy)
    store(0, 1, acts_out)

    total = wblock(z)
    for i in range(3):
        wcopy(i, peer_z[i]).wait_recv()
        total = total + wrecv[peer_z[i]].astype(F32)
    wg_s[...] = total * (TICKS * ROWS * NDP) ** -0.5
    last = pltpu.make_async_copy(wg_s, wgrad_out.at[0], st_sem.at[4])
    last.start()
    drain()
    for copy in stores + [last]:
        copy.wait()


def solution(mesh):
    sections = mesh.shape["section"]
    in_specs = (
        P(None, "dp", None),
        P("section", "dp", None),
        P(None, "dp", None),
        P("section", "dp", None),
        P("section", None, "dp", None),
        P("section", "dp", "cores"),
        P("section", "cores", "dp"),
        P("dp", None),
        P("dp", None),
        P("dp", None, None, None),
        P("dp", None, None, None),
    )
    out_specs = (
        P("section", None, ("dp", "cores"), None),
        P("section", None, ("dp", "cores"), None),
        P("section", "cores", "dp"),
    )
    dma, vmem = pltpu.SemaphoreType.DMA, pltpu.VMEM
    scratch = [
        vmem((HEADS, D, WIDE), BF16),
        vmem((HEADS * HEAD, D), BF16),
        vmem((TICKS, NX, ROWS, HEADS * HEAD), BF16),
        vmem((TICKS, NX, ROWS, NZ * SHARD), BF16),
        vmem((TICKS, ROWS, D), BF16),
        vmem((TICKS, ROWS, D), BF16),
        vmem((TICKS, ROWS, D), BF16),
        vmem((TICKS, ROWS, D), BF16),
        vmem((TICKS, ROWS, D), BF16),
        vmem((3 * ROWS, D), BF16),
        vmem((3 * ROWS, WIDE), F32),
        vmem((ROWS, D), F32),
        vmem((ROWS, D), F32),
        vmem((ROWS, HEADS * HEAD), BF16),
        vmem((ROWS, HEADS * HEAD), F32),
        vmem((HEADS, ROWS, WIDE), F32),
        vmem((TICKS, HEADS, ROWS, WIDE), F32),
        vmem((TICKS, HEADS, ROWS, HEAD), F32),
        vmem((TICKS, HEADS, ROWS, HEAD), F32),
        vmem((TICKS, HEADS, ROWS, HEAD), F32),
        vmem((TICKS, HEADS, ROWS, HEAD), BF16),
        vmem((TICKS, HEADS, ROWS, HEAD), BF16),
        vmem((TICKS, HEADS, ROWS, HEAD), BF16),
        vmem((TICKS, HEADS, ROWS, ROWS), BF16),
        vmem((TICKS, HEADS, ROWS, ROWS), F32),
        vmem((2 * TICKS, ROWS, ROWS), F32),
        vmem((2 * TICKS, HALF, D), BF16),
        vmem((2 * TICKS, HALF, D), BF16),
        vmem((2, TICKS, HALF, D), BF16),
        vmem((HEADS * HEAD, SHARD), F32),
        vmem((HEADS * HEAD, NZ * SHARD), F32),
        vmem((3, HEADS * HEAD, SHARD), BF16),
        vmem((NZ, HEADS * HEAD, SHARD), BF16),
        dma((10,)),
        dma((HEADS + 3, NDP)),
        dma((HEADS + 3, 17)),
        dma((4,)),
        dma((4,)),
        dma((2, PARTS)),
        dma((2, PARTS)),
        dma((2, PARTS)),
        dma((2, PARTS)),
        dma((TICKS, NX, NZ)),
        dma((TICKS, NX, NZ)),
        dma((TICKS, NX)),
        dma((TICKS, NX)),
        dma((3,)),
        dma((NZ,)),
        dma((5,)),
    ]

    def per_device(*args):
        marks = [jnp.transpose(m, (0, 2, 3, 1)) for m in args[9:]]
        any_spec = pl.BlockSpec(memory_space=pl.ANY)
        smem_spec = pl.BlockSpec(memory_space=pltpu.SMEM)

        def body(*refs):
            kernel(sections, *refs)

        results = pl.pallas_call(
            body,
            out_shape=(
                jax.ShapeDtypeStruct((1, TICKS, HALF, D), BF16),
                jax.ShapeDtypeStruct((1, TICKS, HALF, D), BF16),
                jax.ShapeDtypeStruct((1, HEADS * HEAD, SHARD), F32),
            ),
            in_specs=[any_spec] * 7 + [smem_spec] * 4,
            out_specs=(any_spec,) * 3,
            scratch_shapes=scratch,
            compiler_params=pltpu.CompilerParams(
                collective_id=0, has_side_effects=True, vmem_limit_bytes=58 * 2**20
            ),
            name="window",
        )(*args[:9], *marks)

        def put(*refs):
            held, sems = refs[6:9], refs[9]
            loads = [pltpu.make_async_copy(refs[i], held[i], sems.at[i]) for i in range(3)]
            stores = [pltpu.make_async_copy(held[i], refs[3 + i], sems.at[3 + i]) for i in range(3)]
            for copy in loads:
                copy.start()
            for load, keep in zip(loads, stores):
                load.wait()
                keep.start()
            for copy in stores:
                copy.wait()

        return pl.pallas_call(
            put,
            out_shape=tuple(jax.ShapeDtypeStruct(r.shape, r.dtype) for r in results),
            in_specs=[any_spec] * 3,
            out_specs=(any_spec,) * 3,
            scratch_shapes=[vmem(r.shape, r.dtype) for r in results] + [dma((6,))],
            name="put",
        )(*results)

    return jax.shard_map(
        per_device, mesh=mesh, in_specs=in_specs, out_specs=out_specs, check_vma=False
    )
```

```python
import jax
import jax.numpy as jnp
from jax import lax
from jax.experimental import pallas as pl
from jax.experimental.pallas import tpu as pltpu
from jax.sharding import PartitionSpec as P

HEAD = 128
AHEAD_AFTER = 0
HEADS = 4
WIDE = 4 * HEAD
BLOCK = 24
BLOCKS = 4
ROWS = BLOCK * BLOCKS
HALF = ROWS // 2
D = 2048
TICKS = 2
NZ, NX = 4, 4
NDP = NZ * NX
PARTS = D // WIDE
SHARD = D // NDP
EPSILON = 1e-06
SCALE = HEAD**-0.5
MESH = pl.DeviceIdType.MESH
F32, BF16 = jnp.float32, jnp.bfloat16

NT = (((1,), (1,)), ((), ()))
TN = (((0,), (0,)), ((), ()))


def sigmoid(v):
    return 1.0 / (1.0 + jnp.exp(-v))


def dot(a, b, dims=(((1,), (0,)), ((), ()))):
    return lax.dot_general(a, b, dims, preferred_element_type=F32)


def inverse_rms(v):
    return lax.rsqrt(jnp.mean(v * v, axis=-1, keepdims=True) + EPSILON)


def keep_count(blocks, marks, history):
    i = lax.broadcasted_iota(jnp.int32, (ROWS, ROWS), 0)
    j = lax.broadcasted_iota(jnp.int32, (ROWS, ROWS), 1)

    def owner(p):
        return sum((p >= BLOCK * b).astype(jnp.int32) for b in range(1, BLOCKS))

    bi, bj = owner(i), owner(j)
    spread = (bi == bj).astype(jnp.int32)
    for a in range(1, BLOCKS):
        for b in range(a):
            here = ((bi == a) & (bj == b)).astype(jnp.int32)
            spread = spread + here * marks[0, a, b, history]
    live = jnp.full((ROWS, ROWS), blocks[0, history] * BLOCK, jnp.int32)
    keep = (spread > 0) & (j <= i) & (i < live) & (j < live)
    return jnp.where(keep, 1.0 / live.astype(F32), 0.0)


def kernel(
    sections,
    arrivals,
    in_flight,
    cotangent,
    grad_flight,
    stashed,
    in_weight,
    out_weight,
    f_blocks,
    b_blocks,
    f_marks,
    b_marks,
    acts_out,
    grads_out,
    wgrad_out,
    win,
    wout,
    gat,
    gcol,
    xin,
    gin,
    xsrc,
    gsrc,
    stash,
    xn,
    u_s,
    part,
    dxn,
    dgat,
    dgat_s,
    u_next,
    dsil_s,
    gate_s,
    norm_s,
    rs_s,
    v_s,
    q_s,
    k_s,
    p_s,
    dsc_s,
    keep_s,
    esend,
    erecv,
    outs,
    wg_s,
    wsum,
    wsend,
    wrecv,
    load_sem,
    ag_recv,
    ag_send,
    ex_send,
    ex_recv,
    sec_send,
    sec_recv,
    fw_send,
    fw_recv,
    a2a_send,
    a2a_recv,
    pair_send,
    pair_recv,
    w_send,
    w_recv,
    st_sem,
):
    s = lax.axis_index("section")
    me = lax.axis_index("dp")
    c = lax.axis_index("cores")
    z, x = me // NX, me % NX
    right, left, across = (x + 1) % NX, (x + NX - 1) % NX, (x + 2) % NX
    near_z = z - 1 + 2 * ((NZ - 1 - z) // (NZ - 1))
    far_z = (NZ - 1) * (1 - z // 2)
    peer_z = (near_z, 6 - z - near_z - far_z, far_z)
    zs = (z,) + peer_z
    inner = z % (NZ - 1) != 0
    hop_z = (z + 1, z - 1, (NZ - 1) * (z - 1))
    ahead, behind = (s + 1) % sections, (s + sections - 1) % sections
    mine, other = pl.multiple_of(c * HALF, 16), pl.multiple_of((1 - c) * HALF, 16)

    barrier = pltpu.get_barrier_semaphore()
    for k in range(1, NDP):
        pl.semaphore_signal(barrier, inc=1, device_id=(s, (me + k) % NDP, c), device_id_type=MESH)
    pl.semaphore_signal(barrier, inc=1, device_id=(s, me, 1 - c), device_id_type=MESH)
    pl.semaphore_signal(barrier, inc=1, device_id=(ahead, me, c), device_id_type=MESH)
    pl.semaphore_signal(barrier, inc=1, device_id=(behind, me, c), device_id_type=MESH)

    def chunk(n, owner):
        if n == HEADS:
            return wout.at[:, pl.ds(pl.multiple_of(owner * SHARD, SHARD), SHARD)]
        if n == HEADS + 1:
            return gat.at[0, owner % NX]
        if n == HEADS + 2:
            return gat.at[1, owner % NX]
        return win.at[n, pl.ds(pl.multiple_of(owner * SHARD, SHARD), SHARD), :]

    loads = []
    for h in range(HEADS):
        loads.append((in_weight.at[0, :, pl.ds(h * WIDE, WIDE)], chunk(h, me)))
    loads.append((out_weight.at[0], chunk(HEADS, me)))
    loads += [
        (stashed.at[0], stash),
        (arrivals, xsrc),
        (in_flight.at[0], xin.at[0]),
        (cotangent, gsrc),
        (grad_flight.at[0], gin.at[0]),
    ]
    loads = [pltpu.make_async_copy(a, b, load_sem.at[i]) for i, (a, b) in enumerate(loads)]
    for copy in loads:
        copy.start()

    def remote(src, dst, send, recv, to):
        return pltpu.make_async_remote_copy(
            src_ref=src, dst_ref=dst, send_sem=send, recv_sem=recv, device_id=to, device_id_type=MESH
        )

    sent = []

    def start(copy, cond=None):
        if cond is None:
            copy.start()
        else:
            pl.when(cond)(copy.start)
        sent.append((copy, cond))

    def ag(n, owner, slot, to_z, to_x):
        block = chunk(n, owner)
        return remote(
            block, block, ag_send.at[n, slot], ag_recv.at[n, owner], (s, to_z * NX + to_x, c)
        )

    def push(n, owner, slot, to_z, to_x, cond=None):
        start(ag(n, owner, slot, to_z, to_x), cond)

    def arrive(n, owner):
        ag(n, owner, 0, z, right).wait_recv()

    def begin(n):
        push(n, me, 0, z, right)
        push(n, me, 1, z, left)
        push(n, me, 2, z + 1, x, z < NZ - 1)
        push(n, me, 3, z - 1, x, z > 0)

    def spread(n):
        for i in range(3):
            owner = peer_z[i] * NX + x
            arrive(n, owner)
            push(n, owner, 10 + i, hop_z[i], x, inner)
            push(n, owner, 4 + 2 * i, z, right)
            push(n, owner, 5 + 2 * i, z, left)

    def forward(n):
        for i in range(4):
            from_left, from_right = zs[i] * NX + left, zs[i] * NX + right
            if i in (0, 3):
                arrive(n, from_left)
                push(n, from_left, 13 + i, z, right)
                arrive(n, from_right)
            else:
                arrive(n, from_right)
                push(n, from_right, 13 + i, z, left)
                arrive(n, from_left)

    def finish(n):
        for i in range(4):
            arrive(n, zs[i] * NX + across)

    xs = (x, right, left, across)
    OUT, GATED = HEADS, HEADS + 1

    def ring(n):
        for i in range(1, NX):
            push(n, me, i - 1, z, xs[i])

    def ring_both():
        for t in range(TICKS):
            push(GATED + t, me, 0, z, right)
            push(GATED + t, me, 1, z, left)

    def pass_ring():
        for t in range(TICKS):
            arrive(GATED + t, z * NX + (left, right)[t])
            push(GATED + t, z * NX + (left, right)[t], 2, z, (right, left)[t])

    def line(i):
        owner = z * NX + xs[i]
        if i:
            arrive(OUT, owner)
        for k in range(3):
            push(OUT, owner, 3 + 3 * i + k, peer_z[k], xs[0])

    def finish_line():
        for i in range(NX):
            for k in range(3):
                arrive(OUT, peer_z[k] * NX + xs[i])

    def finish_ring():
        for t in range(TICKS):
            arrive(GATED + t, z * NX + (right, left)[t])
            arrive(GATED + t, z * NX + across)

    loads[0].wait()
    pl.semaphore_wait(barrier, NDP - 1 + 3)
    begin(0)
    loads[HEADS].wait()
    ring(OUT)
    loads[1].wait()
    begin(1)

    for t in range(TICKS):
        keep_s[t] = keep_count(f_blocks, f_marks, t - s + sections - 1)
        keep_s[2 + t] = keep_count(b_blocks, b_marks, t + s)

    def normed(v):
        v = v.astype(F32)
        return (v * inverse_rms(v)).astype(BF16)

    spread(0)
    line(0)
    for copy in loads[2:HEADS] + loads[HEADS + 1 :]:
        copy.wait()

    xsrc[0] = jnp.where(s == 0, xsrc[0], xin[0])
    gsrc[0] = jnp.where(s == sections - 1, gsrc[0], gin[0])
    xn[0:ROWS] = normed(xsrc[0])
    for t in range(TICKS):
        xn[ROWS * (t + 1) : ROWS * (t + 2)] = normed(stash[t])

    def columns(owner_z, owner_x):
        return pl.ds(pl.multiple_of((owner_z * NX + owner_x) * SHARD, SHARD), SHARD)

    def a2a(t, i, owner_z, sender):
        return remote(
            gsrc.at[t, pl.ds(mine, HALF), columns(owner_z, xs[i])],
            gcol.at[t, sender, pl.ds(mine, HALF), pl.ds(owner_z * SHARD, SHARD)],
            a2a_send.at[t, i, owner_z],
            a2a_recv.at[t, sender, owner_z],
            (s, z * NX + xs[i], c),
        )

    def a2a_start(t, *only):
        for owner_z in only or range(NZ):
            for i in range(1, NX):
                start(a2a(t, i, owner_z, x))

    def pair(t, i):
        half = gcol.at[t, xs[i], pl.ds(mine, HALF)]
        return remote(half, half, pair_send.at[t, i], pair_recv.at[t, i], (s, me, 1 - c))

    def a2a_pass(t):
        for i in range(1, NX):
            for owner_z in range(NZ):
                a2a(t, i, owner_z, xs[i]).wait_recv()
            start(pair(t, i))
        for owner_z in range(NZ):
            gcol[t, x, :, owner_z * SHARD : (owner_z + 1) * SHARD] = gsrc[t, :, columns(owner_z, x)]

    def a2a_wait(t):
        for i in range(1, NX):
            pair(t, i).wait_recv()

    def heads_forward(u, keep):
        sg = sigmoid(u)
        act = u * sg
        gate = act[:, :HEAD]
        v = act[:, HEAD : 2 * HEAD].astype(BF16)
        q = act[:, 2 * HEAD : 3 * HEAD].astype(BF16)
        k = act[:, 3 * HEAD :].astype(BF16)
        scores = dot(q, k, NT) * SCALE
        ss = sigmoid(scores)
        probs = (scores * ss * keep).astype(BF16)
        mixed = dot(probs, v)
        rs = inverse_rms(mixed)
        norm = mixed * rs
        return (norm * gate).astype(BF16), (sg, gate, v, q, k, scores, ss, probs, rs, norm)

    def ahead_part(t, h, u):
        gated, _ = heads_forward(u, keep_s[t])
        more = dot(gated, wout[h * HEAD : (h + 1) * HEAD, :])
        if h == 0:
            part[...] = more
        else:
            part[...] += more

    def back_first(t, h, u):
        keep = keep_s[2 + t]
        gated, (sg, gate, v, q, k, scores, ss, probs, rs, norm) = heads_forward(u, keep)
        gat[t, x, :, h * HEAD : (h + 1) * HEAD] = gated
        dsil_s[t, h] = sg * (1.0 + u * (1.0 - sg))
        gate_s[t, h] = gate
        norm_s[t, h] = norm
        rs_s[t, h] = jnp.broadcast_to(rs, (ROWS, HEAD))
        v_s[t, h] = v
        q_s[t, h] = q
        k_s[t, h] = k
        p_s[t, h] = probs
        dsc_s[t, h] = keep * ss * (1.0 + scores * (1.0 - ss)) * SCALE

    def back_second(t, h):
        dg = dgat[:, h * HEAD : (h + 1) * HEAD].astype(F32)
        norm = norm_s[t, h]
        dn = dg * gate_s[t, h]
        dgate = dg * norm
        dm = (rs_s[t, h] * (dn - norm * jnp.mean(dn * norm, axis=-1, keepdims=True))).astype(BF16)
        dp = dot(dm, v_s[t, h], NT)
        dv = dot(p_s[t, h], dm, TN)
        ds = (dp * dsc_s[t, h]).astype(BF16)
        dq = dot(ds, k_s[t, h])
        dk = dot(ds, q_s[t, h], TN)
        du = (jnp.concatenate([dgate, dv, dq, dk], axis=1) * dsil_s[t, h]).astype(BF16)
        more = dot(du, win[h], NT)
        if h == 0:
            dxn[...] = more
        else:
            dxn[...] += more

    def gated_grad(t):
        dgat[...] = dot(gsrc[t], wout[...], NT).astype(BF16)

    def project(h):
        u_s[...] = dot(xn[...], win[h])

    def u_of(i):
        return u_s[ROWS * i : ROWS * (i + 1)]

    def exchange(i, total):
        esend[i] = total[pl.ds(other, HALF)].astype(BF16)
        copy = remote(esend.at[i], erecv.at[i], ex_send.at[i], ex_recv.at[i], (s, me, 1 - c))
        start(copy)
        return copy

    def ahead_end(t, copy):
        copy.wait_recv()
        out = (
            xsrc[t, pl.ds(mine, HALF)].astype(F32)
            + part[pl.ds(mine, HALF)]
            + erecv[t].astype(F32)
        )
        outs[0, t] = out.astype(BF16)

    def back_end(t, copy):
        copy.wait_recv()
        d = dxn[pl.ds(mine, HALF)] + erecv[2 + t].astype(F32)
        saved = stash[t, pl.ds(mine, HALF)].astype(F32)
        root = inverse_rms(saved)
        saved = saved * root
        back = root * (d - saved * jnp.mean(d * saved, axis=-1, keepdims=True))
        outs[1, t] = (gsrc[t, pl.ds(mine, HALF)].astype(F32) + back).astype(BF16)

    stores = []

    def store(i, t, ref):
        copy = pltpu.make_async_copy(outs.at[i, t], ref.at[0, t], st_sem.at[2 * i + t])
        copy.start()
        stores.append(copy)

    def quarter(n):
        return slice(n * WIDE, (n + 1) * WIDE)

    def relay(i, held, to):
        copies = []
        for n in range(PARTS):
            half = held.at[1, pl.ds(mine, HALF), quarter(n)]
            copy = remote(
                outs.at[i, 0, :, quarter(n)], half, sec_send.at[i, n], sec_recv.at[i, n], (to, me, c)
            )
            start(copy)
            copies.append(copy)
        return copies

    def hand_on(i, n, held, far):
        half = held.at[1, pl.ds(mine, HALF), quarter(n)]
        far[n].wait_recv()
        near = remote(half, half, fw_send.at[i, n], fw_recv.at[i, n], (s, me, 1 - c))
        start(near)
        return near

    def drain():
        for copy, cond in sent:
            if cond is None:
                copy.wait_send()
            else:
                pl.when(cond)(copy.wait_send)
        sent.clear()

    gated_ahead = []

    def first(h):
        project(h)
        for t in range(TICKS):
            back_first(t, h, u_of(1 + t))
        gated_ahead.append(heads_forward(u_of(0), keep_s[0])[0])

    forward(0)
    spread(1)
    begin(2)
    line(1)
    finish(0)
    first(0)

    forward(1)
    spread(2)
    begin(3)
    line(2)
    finish(1)
    first(1)

    forward(2)
    spread(3)
    line(3)
    finish(2)
    first(2)

    forward(3)
    finish_line()
    part[...] = dot(jnp.concatenate(gated_ahead, axis=1), wout[: 3 * HEAD, :])
    gated_grad(0)
    for h in range(3):
        back_second(0, h)

    for i in range(NZ):
        arrive(3, zs[i] * NX + across)
        rows = pl.ds(pl.multiple_of(zs[i] * WIDE, WIDE), WIDE)
        more = dot(xn[:, rows], win[3, rows, :])
        if i == 0:
            u_s[...] = more
        else:
            u_s[...] += more
    back_first(0, 3, u_of(1))
    back_second(0, 3)
    back_copy = exchange(2, dxn)
    ahead_part(0, 3, u_of(0))
    ahead_copy = exchange(0, part)
    drained = sent[:-2]
    del sent[:-2]
    back_end(0, back_copy)
    back_far = relay(1, gin, behind)
    store(1, 0, grads_out)
    ahead_end(0, ahead_copy)
    store(0, 0, acts_out)

    back_first(1, 3, u_of(2))
    ring_both()
    a2a_start(0)
    held_back = sent[:]
    sent[:] = drained
    drain()
    sent[:] = held_back

    def weight_term(t):
        return dot(gat[t].reshape(NX * ROWS, HEADS * HEAD), gcol[t].reshape(NX * ROWS, NZ * SHARD), TN)

    def back_quarter(n, near):
        near.wait_recv()
        gsrc[1, pl.ds(other, HALF), quarter(n)] = jnp.where(
            s == sections - 1,
            gsrc[1, pl.ds(other, HALF), quarter(n)],
            gin[1, pl.ds(other, HALF), quarter(n)],
        )
        more = dot(gsrc[1, :, quarter(n)], wout[:, quarter(n)], NT)
        if n == 0:
            dgat_s[...] = more
        else:
            dgat_s[...] += more

    def ahead_quarter(n, near):
        near.wait_recv()
        rows = jnp.where(s == 0, xsrc[1, :, quarter(n)], xin[1, :, quarter(n)])
        xsrc[1, :, quarter(n)] = rows
        for h in range(HEADS):
            more = dot(rows, win[h, quarter(n), :])
            if n == 0:
                u_next[h] = more
            else:
                u_next[h] += more

    nears = []
    for n in range(PARTS):
        nears.append(hand_on(1, n, gin, back_far))
        gsrc[1, pl.ds(mine, HALF), quarter(n)] = jnp.where(
            s == sections - 1,
            gsrc[1, pl.ds(mine, HALF), quarter(n)],
            gin[1, pl.ds(mine, HALF), quarter(n)],
        )
        a2a_start(1, n)
        if n == 1:
            pass_ring()
        if n == 2:
            a2a_pass(0)
        if n == AHEAD_AFTER:
            ahead_far = relay(0, xin, ahead)
        if n:
            back_quarter(n - 1, nears[n - 1])
    back_quarter(PARTS - 1, nears[-1])
    a2a_pass(1)

    finish_ring()
    a2a_wait(0)
    wsum[...] = weight_term(0)
    a2a_wait(1)
    wsum[...] += weight_term(1)

    def wblock(owner_z):
        return wsum[:, pl.ds(pl.multiple_of(owner_z * SHARD, SHARD), SHARD)]

    def wcopy(i, sender):
        return remote(
            wsend.at[i], wrecv.at[sender], w_send.at[i], w_recv.at[sender], (s, peer_z[i] * NX + x, c)
        )

    for i in range(3):
        wsend[i] = wblock(peer_z[i]).astype(BF16)
        start(wcopy(i, z))

    dgat[...] = dgat_s[...].astype(BF16)
    back_second(1, 0)
    back_second(1, 1)
    nears = [hand_on(0, 0, xin, ahead_far)]
    back_second(1, 2)
    nears.append(hand_on(0, 1, xin, ahead_far))
    back_second(1, 3)
    back_copy = exchange(3, dxn)
    ahead_quarter(0, nears[0])
    nears.append(hand_on(0, 2, xin, ahead_far))
    ahead_quarter(1, nears[1])
    nears.append(hand_on(0, 3, xin, ahead_far))
    ahead_quarter(2, nears[2])
    back_end(1, back_copy)
    store(1, 1, grads_out)
    ahead_quarter(3, nears[3])
    root = inverse_rms(xsrc[1].astype(F32))
    gated = [heads_forward(u_next[h] * root, keep_s[1])[0] for h in range(HEADS)]
    part[...] = dot(jnp.concatenate(gated, axis=1), wout[...])
    ahead_copy = exchange(1, part)
    ahead_end(1, ahead_copy)
    store(0, 1, acts_out)

    total = wblock(z)
    for i in range(3):
        wcopy(i, peer_z[i]).wait_recv()
        total = total + wrecv[peer_z[i]].astype(F32)
    wg_s[...] = total * (TICKS * ROWS * NDP) ** -0.5
    last = pltpu.make_async_copy(wg_s, wgrad_out.at[0], st_sem.at[4])
    last.start()
    drain()
    for copy in stores + [last]:
        copy.wait()


def solution(mesh):
    sections = mesh.shape["section"]
    in_specs = (
        P(None, "dp", None),
        P("section", "dp", None),
        P(None, "dp", None),
        P("section", "dp", None),
        P("section", None, "dp", None),
        P("section", "dp", "cores"),
        P("section", "cores", "dp"),
        P("dp", None),
        P("dp", None),
        P("dp", None, None, None),
        P("dp", None, None, None),
    )
    out_specs = (
        P("section", None, ("dp", "cores"), None),
        P("section", None, ("dp", "cores"), None),
        P("section", "cores", "dp"),
    )
    dma, vmem = pltpu.SemaphoreType.DMA, pltpu.VMEM
    scratch = [
        vmem((HEADS, D, WIDE), BF16),
        vmem((HEADS * HEAD, D), BF16),
        vmem((TICKS, NX, ROWS, HEADS * HEAD), BF16),
        vmem((TICKS, NX, ROWS, NZ * SHARD), BF16),
        vmem((TICKS, ROWS, D), BF16),
        vmem((TICKS, ROWS, D), BF16),
        vmem((TICKS, ROWS, D), BF16),
        vmem((TICKS, ROWS, D), BF16),
        vmem((TICKS, ROWS, D), BF16),
        vmem((3 * ROWS, D), BF16),
        vmem((3 * ROWS, WIDE), F32),
        vmem((ROWS, D), F32),
        vmem((ROWS, D), F32),
        vmem((ROWS, HEADS * HEAD), BF16),
        vmem((ROWS, HEADS * HEAD), F32),
        vmem((HEADS, ROWS, WIDE), F32),
        vmem((TICKS, HEADS, ROWS, WIDE), F32),
        vmem((TICKS, HEADS, ROWS, HEAD), F32),
        vmem((TICKS, HEADS, ROWS, HEAD), F32),
        vmem((TICKS, HEADS, ROWS, HEAD), F32),
        vmem((TICKS, HEADS, ROWS, HEAD), BF16),
        vmem((TICKS, HEADS, ROWS, HEAD), BF16),
        vmem((TICKS, HEADS, ROWS, HEAD), BF16),
        vmem((TICKS, HEADS, ROWS, ROWS), BF16),
        vmem((TICKS, HEADS, ROWS, ROWS), F32),
        vmem((2 * TICKS, ROWS, ROWS), F32),
        vmem((2 * TICKS, HALF, D), BF16),
        vmem((2 * TICKS, HALF, D), BF16),
        vmem((2, TICKS, HALF, D), BF16),
        vmem((HEADS * HEAD, SHARD), F32),
        vmem((HEADS * HEAD, NZ * SHARD), F32),
        vmem((3, HEADS * HEAD, SHARD), BF16),
        vmem((NZ, HEADS * HEAD, SHARD), BF16),
        dma((10,)),
        dma((HEADS + 3, NDP)),
        dma((HEADS + 3, 17)),
        dma((4,)),
        dma((4,)),
        dma((2, PARTS)),
        dma((2, PARTS)),
        dma((2, PARTS)),
        dma((2, PARTS)),
        dma((TICKS, NX, NZ)),
        dma((TICKS, NX, NZ)),
        dma((TICKS, NX)),
        dma((TICKS, NX)),
        dma((3,)),
        dma((NZ,)),
        dma((5,)),
    ]

    def per_device(*args):
        marks = [jnp.transpose(m, (0, 2, 3, 1)) for m in args[9:]]
        any_spec = pl.BlockSpec(memory_space=pl.ANY)
        smem_spec = pl.BlockSpec(memory_space=pltpu.SMEM)

        def body(*refs):
            kernel(sections, *refs)

        results = pl.pallas_call(
            body,
            out_shape=(
                jax.ShapeDtypeStruct((1, TICKS, HALF, D), BF16),
                jax.ShapeDtypeStruct((1, TICKS, HALF, D), BF16),
                jax.ShapeDtypeStruct((1, HEADS * HEAD, SHARD), F32),
            ),
            in_specs=[any_spec] * 7 + [smem_spec] * 4,
            out_specs=(any_spec,) * 3,
            scratch_shapes=scratch,
            compiler_params=pltpu.CompilerParams(
                collective_id=0, has_side_effects=True, vmem_limit_bytes=58 * 2**20
            ),
            name="window",
        )(*args[:9], *marks)

        def put(*refs):
            held, sems = refs[6:9], refs[9]
            loads = [pltpu.make_async_copy(refs[i], held[i], sems.at[i]) for i in range(3)]
            stores = [pltpu.make_async_copy(held[i], refs[3 + i], sems.at[3 + i]) for i in range(3)]
            for copy in loads:
                copy.start()
            for load, keep in zip(loads, stores):
                load.wait()
                keep.start()
            for copy in stores:
                copy.wait()

        return pl.pallas_call(
            put,
            out_shape=tuple(jax.ShapeDtypeStruct(r.shape, r.dtype) for r in results),
            in_specs=[any_spec] * 3,
            out_specs=(any_spec,) * 3,
            scratch_shapes=[vmem(r.shape, r.dtype) for r in results] + [dma((6,))],
            name="put",
        )(*results)

    return jax.shard_map(
        per_device, mesh=mesh, in_specs=in_specs, out_specs=out_specs, check_vma=False
    )
```
